256 devices in a mesh: span: 8 (over z), chord: 32 (over x, y, core).
Axes of the slice: x: 4, y: 4, z: 8, core: 2. Of those that a mesh axis runs over, the one named last changes fastest.
Arguments:
- skin_now: float32 [3, 6, 1024, 4096], P(None, None, 'span', 'chord'), may hold values from -6 to 6
- skin_prev: float32 [3, 6, 1024, 4096], P(None, None, 'span', 'chord'), may hold values from -6 to 6
- skin_mat: int32 [6, 1024, 4096], P(None, 'span', 'chord'), may hold values from 0 to 7
- stringer_now: float32 [64, 3, 6, 96, 1024], P('chord', None, None, None, 'span'), as said below
- stringer_prev: float32 [64, 3, 6, 96, 1024], P('chord', None, None, None, 'span'), as said below
- stringer_mat: int32 [64, 6, 96, 1024], P('chord', None, None, 'span'), may hold values from 0 to 7
- owner_slot: int32 [48], replicated, may hold values from 0 to 63, as said below
- rivet_span: int32 [196608], P(('span', 'chord')), may hold values from 0 to 1023, as said below
- rivet_chord: int32 [196608], P(('span', 'chord')), may hold values from 0 to 4095, as said below
- rivet_stringer: int32 [196608], P(('span', 'chord')), may hold values from 0 to 47, as said below
- rivet_cell: int32 [196608], P(('span', 'chord')), may hold values from 0 to 95
- rivet_stiff: float32 [196608], P(('span', 'chord')), may hold values from 0.5 to 3
- mat_stiff: float32 [8], replicated, may hold values from 0.5 to 2
- mat_coef: float32 [8], replicated, may hold values from 0.04 to 0.16
Outputs:
- skin_out: float32 [3, 6, 1024, 4096], P(None, None, 'span', 'chord')
- stringer_out: float32 [64, 3, 6, 96, 1024], P('chord', None, None, None, 'span')
The draws below stay inside these ranges and needn't reach their ends.
Inputs may be any that keep to these rules, and one draw needn't show every extreme that they name: Distinct slots; stringer s is held in slot owner_slot[s], on chord device owner_slot[s] // 2. `stringer_now`: slots that no stringer holds are zero. `stringer_prev`: slots that no stringer holds are zero. `rivet_span`: the 768 rows of one device (devices in span-major order) lie in that device's span slab. `rivet_chord`: each stringer's rivets lie in its foot, a band of 64 skin chord cells inside one chord device, at foot start + rivet_cell * 64 // 96; feet do not intersect and every chord device holds one or two feet, so the rows of one device put exactly 32 on the skin of each chord device with two feet and half of that on the others. `rivet_stringer`: the 768 rows of one device name every stringer exactly 768 // 48 times.
All inputs are finite; a program needn't handle non-finite values.
Results may differ from the reference program's by a relative error of at most 0.00002.
Values sent between devices are 32-bit elements; how exact they have to be, the bound alone decides.
No kernel may reach another device: no remote copies, remote signals or barrier semaphores. Data moves between devices by JAX's collectives and lax.ppermute only.
A program may use at most 128 MiB of HBM per device.

```python
import math
import jax
import jax.numpy as jnp
from jax import lax

SP_DEV = 128
CH_DEV = 128
SCELL = 96
THK = 6
RIV_DEV = 768
STEPS = 2
MATS = 8
SPAN = 1024
CHORD = 4096
STRINGERS = 48
SLOTS = 64
RIVETS = 196608
N_SPAN = 8
N_CHORD = 32


def owner_draw(key):
    return jax.random.permutation(key, SLOTS)[:STRINGERS].astype(jnp.int32)


def occupied(key):
    return jnp.zeros((SLOTS,), jnp.float32).at[owner_draw(key)].set(1.0)


def rivet_layout(key):
    foot_key = jax.random.fold_in(key, 41)
    key_order, key_device = jax.random.split(foot_key, 2)
    base_device = jnp.concatenate([jnp.arange(N_CHORD, dtype=jnp.int32), jnp.arange(N_CHORD // 2, dtype=jnp.int32)])
    foot_half = jnp.concatenate([jnp.zeros((N_CHORD,), jnp.int32), jnp.ones((N_CHORD // 2,), jnp.int32)])
    order = jax.random.permutation(key_order, STRINGERS)
    device_label = jax.random.permutation(key_device, N_CHORD).astype(jnp.int32)
    foot_device = device_label[base_device[order]]
    foot_start = foot_device * CH_DEV + foot_half[order] * (CH_DEV // 2)
    row_key = jax.random.fold_in(key, 43)

    def one_block(block_index):
        block_key = jax.random.fold_in(row_key, block_index)
        key_perm, key_cell = jax.random.split(block_key, 2)
        stringer = jax.random.permutation(key_perm, jnp.arange(RIV_DEV, dtype=jnp.int32) % STRINGERS)
        cell = jax.random.randint(key_cell, (RIV_DEV,), 0, SCELL)
        return (stringer, cell)
    blocks = jnp.arange(N_SPAN * N_CHORD, dtype=jnp.int32)
    stringer, cell = jax.vmap(one_block)(blocks)
    return (stringer.reshape(-1).astype(jnp.int32), cell.reshape(-1).astype(jnp.int32), foot_start.astype(jnp.int32))


def draw_owner_slot(key, part):
    return owner_draw(key)


def draw_stringer_now(key, part):
    occupancy = occupied(key)
    key = jax.random.fold_in(key, 5)
    shape = (SLOTS, 3, THK, SCELL, SPAN)
    values_in = jax.random.normal(key, shape, jnp.float32)
    return values_in * occupancy[:, None, None, None, None]


def draw_stringer_prev(key, part):
    occupancy = occupied(key)
    key = jax.random.fold_in(key, 7)
    shape = (SLOTS, 3, THK, SCELL, SPAN)
    values_in = jax.random.normal(key, shape, jnp.float32)
    return values_in * occupancy[:, None, None, None, None]


def draw_rivet_span(key, part):
    key = jax.random.fold_in(key, 21)

    def one_block(block_index):
        block_key = jax.random.fold_in(key, block_index)
        inside = jax.random.randint(block_key, (RIV_DEV,), 0, SP_DEV)
        return block_index // N_CHORD * SP_DEV + inside
    blocks = jnp.arange(N_SPAN * N_CHORD, dtype=jnp.int32)
    return jax.vmap(one_block)(blocks).reshape(-1).astype(jnp.int32)


def draw_rivet_chord(key, part):
    stringer, cell, foot_start = rivet_layout(key)
    return (foot_start[stringer] + cell * (CH_DEV // 2) // SCELL).astype(jnp.int32)


def draw_rivet_stringer(key, part):
    stringer, cell, foot_start = rivet_layout(key)
    return stringer


def draw_rivet_cell(key, part):
    stringer, cell, foot_start = rivet_layout(key)
    return cell


def set_ends(drawn, stream_key, smallest, top_value):
    extent = drawn.shape
    spot = [jax.random.randint(jax.random.fold_in(stream_key, axis), (), 0, extent[axis]) for axis in range(len(extent))]
    drawn = drawn.at[tuple(spot)].set(smallest)
    longest = extent.index(max(extent))
    spot[longest] = (spot[longest] + 1) % extent[longest]
    return drawn.at[tuple(spot)].set(top_value)


def block_scale(rng, dims, cuts, smallest, high):
    def one(position, blocks):
        steps = jax.random.uniform(jax.random.fold_in(jax.random.fold_in(rng, 6), position), (blocks,), jnp.float32, smallest / len(cuts), high / len(cuts))
        return jnp.repeat(jnp.exp(steps), dims[position] // blocks).reshape((-1,) + (1,) * (len(dims) - position - 1))

    loudness = one(*cuts[0])
    for cut in cuts[1:]:
        loudness = loudness * one(*cut)
    return loudness


def noise(rng, dims, width, limit, cuts=(), kind=jnp.bfloat16):
    values = width * jax.random.normal(rng, dims, jnp.float32)
    if cuts:
        values = values * block_scale(rng, dims, cuts, -0.22, 0.18)
    return jnp.clip(values, -limit, limit).astype(kind)


def setup_inputs(seed: int = 0) -> dict:
    key_list = jax.random.split(jax.random.key(seed), 15)
    return {
        "skin_now": noise(key_list[0], (3, THK, SPAN, CHORD), 1.0, 6.0, ((2, 8), (3, 32)), jnp.float32),
        "skin_prev": noise(key_list[1], (3, THK, SPAN, CHORD), 1.0, 6.0, ((2, 8), (3, 32)), jnp.float32),
        "skin_mat": set_ends(jax.random.randint(key_list[2], (THK, SPAN, CHORD), 0, MATS), jax.random.fold_in(key_list[2], 1), 0, MATS - 1).astype(jnp.int32),
        "stringer_now": draw_stringer_now(jax.random.fold_in(key_list[14], 71), 0),
        "stringer_prev": draw_stringer_prev(jax.random.fold_in(key_list[14], 71), 0),
        "stringer_mat": set_ends(jax.random.randint(key_list[5], (SLOTS, THK, SCELL, SPAN), 0, MATS), jax.random.fold_in(key_list[5], 1), 0, MATS - 1).astype(jnp.int32),
        "owner_slot": draw_owner_slot(jax.random.fold_in(key_list[14], 71), 0),
        "rivet_span": draw_rivet_span(jax.random.fold_in(key_list[14], 71), 0),
        "rivet_chord": draw_rivet_chord(jax.random.fold_in(key_list[14], 71), 0),
        "rivet_stringer": draw_rivet_stringer(jax.random.fold_in(key_list[14], 71), 0),
        "rivet_cell": draw_rivet_cell(jax.random.fold_in(key_list[14], 71), 0),
        "rivet_stiff": jnp.clip(jnp.exp(math.log(3.0) - 1.7917595 * jax.random.uniform(key_list[11], (RIVETS,), jnp.float32) ** block_scale(key_list[11], (RIVETS,), ((0, 256),), -0.2, 0.2)), 0.5, 3.0),
        "mat_stiff": jnp.clip(jnp.exp(jax.random.uniform(key_list[12], (MATS,), jnp.float32, math.log(0.5), math.log(2.0))), 0.5, 2.0),
        "mat_coef": jnp.clip(jnp.exp(jax.random.uniform(key_list[13], (MATS,), jnp.float32, math.log(0.04), math.log(0.16))), 0.04, 0.16),
    }


def bond_stiff(stiff_left, stiff_right):
    return 2.0 * stiff_left * stiff_right / (stiff_left + stiff_right)


def pad_axis(values_in, axis_dim):
    widths = [(0, 0)] * values_in.ndim
    widths[axis_dim] = (1, 1)
    return jnp.pad(values_in, widths)


def side_bonds(stiff_ext, axis_dim, comp_axis):
    inner_count = stiff_ext.shape[axis_dim] - 2
    centre = lax.slice_in_dim(stiff_ext, 1, 1 + inner_count, axis=axis_dim)
    bond_pair = []
    for offset in (0, 2):
        beside = lax.slice_in_dim(stiff_ext, offset, offset + inner_count, axis=axis_dim)
        bond_pair.append(jnp.expand_dims(bond_stiff(centre, beside), comp_axis))
    return bond_pair


def side_pull(field_ext, axis_dim, bond_pair):
    inner_count = field_ext.shape[axis_dim] - 2
    centre = lax.slice_in_dim(field_ext, 1, 1 + inner_count, axis=axis_dim)
    result = bond_pair[0] * (lax.slice_in_dim(field_ext, 0, inner_count, axis=axis_dim) - centre)
    return result + bond_pair[1] * (lax.slice_in_dim(field_ext, 2, 2 + inner_count, axis=axis_dim) - centre)


def grid_pull(field_now, stiffness, comp_axis, spatial_axes):
    pull_sum = jnp.zeros_like(field_now)
    for grid_axis in spatial_axes:
        bond_pair = side_bonds(pad_axis(stiffness, grid_axis), grid_axis, comp_axis)
        pull_sum = pull_sum + side_pull(pad_axis(field_now, grid_axis + 1), grid_axis + 1, bond_pair)
    return pull_sum


def reference(skin_now, skin_prev, skin_mat, stringer_now, stringer_prev, stringer_mat, owner_slot, rivet_span, rivet_chord, rivet_stringer, rivet_cell, rivet_stiff, mat_stiff, mat_coef):
    skin_stiff = jnp.take(mat_stiff, skin_mat)
    skin_coef = jnp.take(mat_coef, skin_mat)
    flange_stiff = jnp.take(mat_stiff, stringer_mat)
    flange_coef = jnp.take(mat_coef, stringer_mat)
    slot_index = jnp.take(owner_slot, rivet_stringer)
    for step_index in range(STEPS):
        skin_disp = skin_now[:, THK - 1][:, rivet_span, rivet_chord]
        flange_disp = stringer_now[:, :, 0][slot_index, :, rivet_cell, rivet_span]
        spring = rivet_stiff[None, :] * (skin_disp - flange_disp.T)
        skin_load = jnp.zeros((3, SPAN, CHORD), jnp.float32).at[:, rivet_span, rivet_chord].add(-spring)
        flange_load = jnp.zeros((SLOTS, 3, SCELL, SPAN), jnp.float32).at[slot_index, :, rivet_cell, rivet_span].add(spring.T)
        skin_pull = grid_pull(skin_now, skin_stiff, 0, (0, 1, 2))
        skin_pull = skin_pull.at[:, THK - 1].add(skin_load)
        skin_next = 2.0 * skin_now - skin_prev + skin_coef[None] * skin_pull
        flange_pull = grid_pull(stringer_now, flange_stiff, 1, (1, 2, 3))
        flange_pull = flange_pull.at[:, :, 0].add(flange_load)
        flange_next = 2.0 * stringer_now - stringer_prev + flange_coef[:, None] * flange_pull
        skin_prev, skin_now = skin_now, skin_next
        stringer_prev, stringer_now = stringer_now, flange_next
    return skin_now, stringer_now
```

```python
import jax
import jax.numpy as jnp
from jax import lax
from jax.experimental import pallas as pl
from jax.experimental.pallas import tpu as pltpu
from jax.sharding import PartitionSpec as P

F32 = jnp.float32
BF16 = jnp.bfloat16
NT = (((1,), (1,)), ((), ()))
TN = (((0,), (0,)), ((), ()))
FIELDS = 7


def iota(shape, dim):
    return lax.broadcasted_iota(jnp.int32, shape, dim)


def two_parts(values):
    high = values.astype(BF16)
    return high, (values - high.astype(F32)).astype(BF16)


def pick(mask, values):
    return jnp.where(mask, values, 0.0).astype(BF16)


def params():
    return pltpu.CompilerParams(vmem_limit_bytes=48 * 1024 * 1024)


def call(body, outs, ins, name, smem=(), flops=0, nbytes=0):
    specs = [
        pl.BlockSpec(memory_space=pltpu.SMEM) if i in smem else pl.BlockSpec(memory_space=pltpu.VMEM)
        for i in range(len(ins))
    ]
    return pl.pallas_call(
        body,
        out_shape=[jax.ShapeDtypeStruct(s, F32) for s in outs],
        in_specs=specs,
        out_specs=[pl.BlockSpec(memory_space=pltpu.VMEM) for _ in outs],
        compiler_params=params(),
        cost_estimate=pl.CostEstimate(flops=flops, bytes_accessed=nbytes, transcendentals=0),
        name=name,
    )(*ins)


def tables(stiff_ref, coef_ref):
    half = [0.5 / jnp.full((1, 128), stiff_ref[m], F32) for m in range(8)]
    return half, [coef_ref[m] for m in range(8)]


def half_of(mat, tabs):
    out = jnp.broadcast_to(tabs[0][0], mat.shape)
    for m in range(1, 8):
        out = jnp.where(mat == m, tabs[0][m], out)
    return out


def half_coef(mat, tabs):
    half = jnp.broadcast_to(tabs[0][0], mat.shape)
    coef = jnp.full(mat.shape, tabs[1][0], F32)
    for m in range(1, 8):
        same = mat == m
        half = jnp.where(same, tabs[0][m], half)
        coef = jnp.where(same, tabs[1][m], coef)
    return half, coef


def edge_bond(half, beside):
    return jnp.where(beside > 0.0, 1.0 / (half + beside), 0.0)


def layer_bonds(half, rows, cols):
    count = half.shape[0]
    row, lane = iota(half.shape, 0), iota(half.shape, 1)
    below = pltpu.roll(half, count - 1, 0)
    down = 1.0 / (half + below)
    if rows is None:
        down = jnp.where(row == count - 1, 0.0, down)
        first = None
    else:
        first = edge_bond(half[0:1], rows[0])
        last = edge_bond(half[count - 1 : count], rows[1])
        down = jnp.where(row == count - 1, last, down)
    across = 1.0 / (half + pltpu.roll(half, 127, 1))
    left = edge_bond(half[:, 0:1], cols[0])
    right = edge_bond(half[:, 127:128], cols[1])
    across = jnp.where(lane == 127, right, across)
    return down, first, across, left


def layer_pull(cells, bonds, rows, cols):
    down, first, across, left = bonds
    count = cells.shape[0]
    row, lane = iota(cells.shape, 0), iota(cells.shape, 1)
    below = pltpu.roll(cells, count - 1, 0)
    if rows is not None:
        below = jnp.where(row == count - 1, rows[1], below)
    flux = down * (below - cells)
    above = pltpu.roll(flux, 1, 0)
    if rows is not None:
        above = jnp.where(row == 0, first * (cells[0:1] - rows[0]), above)
    beside = jnp.where(lane == 127, cols[1], pltpu.roll(cells, 127, 1))
    side = across * (beside - cells)
    before = jnp.where(lane == 0, left * (cells[:, 0:1] - cols[0]), pltpu.roll(side, 1, 1))
    return (flux - above) + (side - before)


def update_layer(layer, comps, now, prev, half, coef, thick, rows, cols, half_rows, half_cols, extra, put):
    bonds = layer_bonds(half, half_rows, half_cols)
    for comp in range(comps):
        cells = now(comp, layer)
        pull = layer_pull(cells, bonds, rows(comp), cols(comp))
        if layer < 5:
            pull = pull + thick(layer) * (now(comp, layer + 1) - cells)
        if layer > 0:
            pull = pull + thick(layer - 1) * (now(comp, layer - 1) - cells)
        if extra is not None:
            pull = pull + extra(comp)
        put(comp, 2.0 * cells - prev(comp, layer) + coef * pull)


def skin_rows(before, after, index):
    return before[index : index + 1, :], after[index : index + 1, :]


def lanes_of(before, after, index):
    return before[:, index : index + 1], after[:, index : index + 1]


def prep_body(span_ref, chord_ref, stringer_ref, cell_ref, stiff_ref, owner_ref, out_ref, match_ref):
    def row_of(ref):
        return ref[...]

    span, chord, stringer = row_of(span_ref), row_of(chord_ref), row_of(stringer_ref)
    cell, stiff = row_of(cell_ref), row_of(stiff_ref)
    count = span.shape[1]
    chunks = count // 128
    same = iota((48, count), 0) == stringer
    owner = owner_ref[...]
    slot = jnp.sum(jnp.where(same, owner, 0).astype(F32), axis=0, keepdims=True).astype(jnp.int32)
    foot = (chord - (((2 * cell) * 171) >> 9)) >> 6
    foot_of = jnp.max(jnp.where(same, foot, 0).astype(F32), axis=1, keepdims=True).astype(jnp.int32)
    slots = iota((48, 64), 1)
    slot_hot = (slots == (owner & 1) * 32 + (owner >> 1)).astype(F32).astype(BF16)
    foot_hot = (slots == (foot_of & 1) * 32 + (foot_of >> 1)).astype(F32).astype(BF16)
    match_ref[0:64, 0:64] = lax.dot_general(foot_hot, slot_hot, TN, preferred_element_type=F32)
    match_ref[64:128, 0:64] = lax.dot_general(slot_hot, foot_hot, TN, preferred_element_type=F32)
    one = same.astype(F32)
    lower = (iota((128, 128), 0) < iota((128, 128), 1)).astype(F32).astype(BF16)
    both = jnp.concatenate([lower, jnp.ones((128, 128), BF16)], axis=1)
    offset = jnp.zeros((48, 128), F32)
    ranks = []
    for k in range(chunks):
        part = one[:, k * 128 : (k + 1) * 128]
        ahead = jnp.dot(part.astype(BF16), both, preferred_element_type=F32)
        ranks.append(jnp.sum(part * (ahead[:, :128] + offset), axis=0, keepdims=True))
        offset = offset + ahead[:, 128:]
    rank = jnp.concatenate(ranks, axis=1).astype(jnp.int32)
    place = iota((128, count), 0)
    place = place == jnp.where(
        place < 64, (slot & 1) * 32 + (slot >> 1), 64 + (foot & 1) * 32 + (foot >> 1)
    )
    place = place.astype(F32).astype(BF16)
    order = iota((16, count), 0) == rank
    high = stiff.astype(BF16).astype(F32)
    rest = stiff - high
    middle = rest.astype(BF16).astype(F32)
    fields = [cell.astype(F32), (span & 127).astype(F32), (chord & 127).astype(F32), high, middle, rest - middle]
    rows = jnp.concatenate([pick(order, f) for f in fields], axis=0)
    got = lax.dot_general(place, rows, NT, preferred_element_type=F32)
    for side in range(2):
        index, weight = [], []
        for p in range(2):
            part = got[side * 64 + p * 32 : side * 64 + p * 32 + 32]
            where_, across = part[:, 0:16], part[:, 16:32]
            if side == 1:
                where_, across = part[:, 16:32], part[:, 32:48]
            index.append(where_ * 128.0 + across)
            weight.append(part[:, 48:64] + part[:, 64:80] + part[:, 80:96])
        out_ref[:, side * 64 : side * 64 + 64] = jnp.concatenate(index + weight, axis=1)


def halo_body(stiff_ref, coef_ref, skin_ref, mat_ref, str_ref, smat_ref, last_ref, first_ref, right_ref, left_ref):
    tabs = tables(stiff_ref, coef_ref)
    lane = iota((128, 128), 1)
    slane = iota((96, 128), 1)
    right = jnp.zeros((128, 128), F32)
    left = jnp.zeros((128, 128), F32)
    for l in range(6):
        half = half_of(mat_ref[l], tabs)
        for f, tile in [(c * 6 + l, skin_ref[c, l]) for c in range(3)] + [(18 + l, half)]:
            last_ref[f : f + 1, :] = tile[127:128, :]
            first_ref[f : f + 1, :] = tile[0:1, :]
            right = jnp.where(lane == f, tile[:, 127:128], right)
            left = jnp.where(lane == f, tile[:, 0:1], left)
    right_ref[...] = right
    left_ref[...] = left
    last = jnp.zeros((96, 128), F32)
    first = jnp.zeros((96, 128), F32)
    for p in range(2):
        for t in range(6):
            half = half_of(smat_ref[p, t], tabs)
            tiles = [((p * 3 + c) * 6 + t, str_ref[p, c, t]) for c in range(3)] + [(36 + p * 6 + t, half)]
            for f, tile in tiles:
                last = jnp.where(slane == f, tile[:, 127:128], last)
                first = jnp.where(slane == f, tile[:, 0:1], first)
    last_ref[24:120, :] = last
    first_ref[24:120, :] = first


def exchange(last, first, right, left):
    up = [(i, i + 1) for i in range(lax.axis_size("span") - 1)]
    side = [(i, i + 1) for i in range(lax.axis_size("chord") - 1)]
    back = lambda pairs: [(b, a) for a, b in pairs]
    before = lax.ppermute(last, "span", up)
    after = lax.ppermute(first, "span", back(up))
    lefts = lax.ppermute(right, "chord", side)
    rights = lax.ppermute(left, "chord", back(side))
    return before, after, lefts, rights


def row_lists(index):
    return jnp.concatenate([index[q * 8 : q * 8 + 8, :] for q in range(4)], axis=1)


def one_row(values):
    return jnp.concatenate([values[a : a + 1, :] for a in range(8)], axis=1)


def hots(rows_ref):
    text = one_row(row_lists(rows_ref[:, 0:32])).astype(jnp.int32)
    tk = one_row(row_lists(rows_ref[:, 32:64]))
    sext = one_row(row_lists(rows_ref[:, 64:96])).astype(jnp.int32)
    sk = one_row(row_lists(rows_ref[:, 96:128]))
    slot = ((iota((1, 1024), 1) >> 4) & 1) * 128
    t_row = iota((96, 1024), 0) == (text >> 7)
    t_lane = (iota((256, 1024), 0) == (text & 127) + slot).astype(F32).astype(BF16)
    s_row = iota((128, 1024), 0) == (sext >> 7)
    s_lane = (iota((128, 1024), 0) == (sext & 127)).astype(F32).astype(BF16)
    return (t_row, t_lane, tk), (s_row, s_lane, sk)


def spread(row_mask, lane_hot, values):
    high, low = two_parts(values)
    left = jnp.concatenate([pick(row_mask, high.astype(F32)), pick(row_mask, low.astype(F32))], axis=1)
    right = jnp.concatenate([lane_hot, lane_hot], axis=1)
    return lax.dot_general(left, right, NT, preferred_element_type=F32)


def fetch(row_mask, lane_hot2, cells):
    high, low = two_parts(cells)
    wide = jnp.dot(jnp.concatenate([high, low], axis=1), lane_hot2, preferred_element_type=F32)
    return jnp.sum(jnp.where(row_mask, wide, 0.0), axis=0, keepdims=True)


def as_lanes(row):
    return jnp.concatenate([row[:, a * 128 : (a + 1) * 128] for a in range(8)], axis=0)


def gather_body(
    stiff_ref, coef_ref, rows_ref, skin_ref, skin_prev_ref, mat_ref, str_ref, str_prev_ref, smat_ref,
    before_ref, after_ref, lefts_ref, rights_ref,
    out_ref, ks_ref, ps_ref, cs_ref, kt_ref, pt_ref, ct_ref,
):
    tabs = tables(stiff_ref, coef_ref)
    (t_row, t_lane, tk), (s_row, s_lane, sk) = hots(rows_ref)
    k_skin = spread(s_row, s_lane, sk)
    k_str = spread(t_row, t_lane, tk)
    ks_ref[...] = k_skin
    kt_ref[...] = k_str
    under = half_of(mat_ref[0], tabs)
    half, coef = half_coef(mat_ref[1], tabs)
    bt = 1.0 / (half + under)
    skin_fields = [skin_ref[c, 1] for c in range(3)]
    cs_ref[...] = coef

    def put_skin(c, value):
        moved = value - coef * k_skin * skin_fields[c]
        ps_ref[c] = moved

    update_layer(
        5, 3, lambda c, l: skin_ref[c, l - 4], lambda c, l: skin_prev_ref[c, 0], half, coef, lambda l: bt,
        lambda c: skin_rows(before_ref, after_ref, c * 6 + 5), lambda c: lanes_of(lefts_ref, rights_ref, c * 6 + 5),
        skin_rows(before_ref, after_ref, 23), lanes_of(lefts_ref, rights_ref, 23), None, put_skin,
    )
    for p in range(2):
        over = half_of(smat_ref[p, 1], tabs)
        half_t, coef_t = half_coef(smat_ref[p, 0], tabs)
        bt_t = 1.0 / (half_t + over)
        ct_ref[:, p * 128 : p * 128 + 128] = coef_t
        kt = k_str[:, p * 128 : p * 128 + 128]

        def put_str(c, value, p=p, coef_t=coef_t, kt=kt):
            pt_ref[c, :, p * 128 : p * 128 + 128] = value - coef_t * kt * str_ref[p, c, 0]

        def cols(f):
            return before_ref[24:120, f : f + 1], after_ref[24:120, f : f + 1]

        update_layer(
            0, 3, lambda c, l: str_ref[p, c, l], lambda c, l: str_prev_ref[p, c, 0], half_t, coef_t, lambda l: bt_t,
            lambda c: None, lambda c: cols((p * 3 + c) * 6), None, cols(36 + p * 6), None, put_str,
        )
    t_fields = [jnp.concatenate([str_ref[0, c, 0], str_ref[1, c, 0]], axis=1) for c in range(3)]
    t_fields += [pt_ref[c] for c in range(3)] + [ct_ref[...] * k_str]
    s_fields = skin_fields + [ps_ref[c] for c in range(3)] + [coef]
    t_two = jnp.concatenate([t_lane, t_lane], axis=0)
    s_two = jnp.concatenate([s_lane, s_lane], axis=0)
    got = [as_lanes(fetch(t_row, t_two, f)) for f in t_fields]
    got += [as_lanes(fetch(s_row, s_two, f)) for f in s_fields]
    pad = jnp.zeros((8, 64), F32)
    for q in range(4):
        out_ref[q * 8 : q * 8 + 8, :] = jnp.concatenate([g[:, q * 32 : q * 32 + 32] for g in got] + [pad], axis=1)


def bounce_body(match_ref, got_ref, out_ref):
    got = got_ref[...]
    lane = iota(got.shape, 1)
    zero = (lane & 16) == 0

    def turned(base):
        def part(to, frm):
            m = match_ref[base + to * 32 : base + to * 32 + 32, frm * 32 : frm * 32 + 32]
            return jnp.dot(m, got, preferred_element_type=F32, precision=lax.Precision.HIGHEST)

        a = part(0, 0) + pltpu.roll(part(0, 1), 512 - 16, 1)
        b = part(1, 1) + pltpu.roll(part(1, 0), 16, 1)
        return jnp.where(zero, a, b)

    out_ref[...] = jnp.where(lane < FIELDS * 32, turned(0), turned(64))


def load_body(
    rows_ref, posted_ref, ks_ref, ps_ref, cs_ref, kt_ref, pt_ref, ct_ref, skin_ref, str_ref,
    last_in, first_in, right_in, left_in,
    skin1_ref, sload_ref, str1_ref, tload_ref, last_ref, first_ref, right_ref, left_ref,
):
    (t_row, t_lane, tk), (s_row, s_lane, sk) = hots(rows_ref)

    def sums(side, row_mask, lane_hot, weight, f):
        at = (side * FIELDS + f) * 32
        return spread(row_mask, lane_hot, weight * one_row(row_lists(posted_ref[:, at : at + 32])))

    last_ref[...] = last_in[...]
    first_ref[...] = first_in[...]
    lane = iota((128, 128), 1)
    right, left = right_in[...], left_in[...]
    ks, cs = ks_ref[...], cs_ref[...]
    qs = sums(0, s_row, s_lane, sk, 6)
    for c in range(3):
        now = skin_ref[c, 0]
        new = ps_ref[c] + cs * sums(0, s_row, s_lane, sk, c)
        skin1_ref[c] = new
        sload_ref[c] = sums(0, s_row, s_lane, sk, 3 + c) + qs * now - ks * new
        f = c * 6 + 5
        last_ref[f : f + 1, :] = new[127:128, :]
        first_ref[f : f + 1, :] = new[0:1, :]
        right = jnp.where(lane == f, new[:, 127:128], right)
        left = jnp.where(lane == f, new[:, 0:1], left)
    right_ref[...] = right
    left_ref[...] = left
    kt, ct = kt_ref[...], ct_ref[...]
    qt = sums(1, t_row, t_lane, tk, 6)
    third = iota((96, 256), 0) % 3
    slane = iota((96, 128), 1)
    last, first = last_in[24:120, :], first_in[24:120, :]
    for c in range(3):
        now = jnp.concatenate([str_ref[0, c, 0], str_ref[1, c, 0]], axis=1)
        own = kt * now
        pair = jnp.where(third == 0, pltpu.roll(own, 95, 0), jnp.where(third == 1, pltpu.roll(own, 1, 0), 0.0))
        new = pt_ref[c] + ct * sums(1, t_row, t_lane, tk, c)
        load = sums(1, t_row, t_lane, tk, 3 + c) + qt * (own + pair) - kt * new
        for p in range(2):
            str1_ref[p, c] = new[:, p * 128 : p * 128 + 128]
            tload_ref[p, c] = load[:, p * 128 : p * 128 + 128]
            f = (p * 3 + c) * 6
            last = jnp.where(slane == f, new[:, p * 128 + 127 : p * 128 + 128], last)
            first = jnp.where(slane == f, new[:, p * 128 : p * 128 + 1], first)
    last_ref[24:120, :] = last
    first_ref[24:120, :] = first


def whole_step(tabs, mat_ref, smat_ref, skin, skin_prev, stringer, str_prev, halos, skin_layers, str_layers, skin_load, str_load, put_skin, put_str):
    before_ref, after_ref, lefts_ref, rights_ref, hb_ref, ha_ref, hl_ref, hr_ref = halos
    halves = [half_coef(mat_ref[l], tabs) for l in range(6)]
    bt = [1.0 / (halves[l][0] + halves[l + 1][0]) for l in range(5)]
    for l in skin_layers:
        update_layer(
            l, 3, skin, skin_prev, halves[l][0], halves[l][1], lambda m: bt[m],
            lambda c: skin_rows(before_ref, after_ref, c * 6 + l),
            lambda c: lanes_of(lefts_ref, rights_ref, c * 6 + l),
            skin_rows(hb_ref, ha_ref, 18 + l), lanes_of(hl_ref, hr_ref, 18 + l),
            skin_load if l == 5 else None, lambda c, v: put_skin(c, l, v),
        )
    for p in range(2):
        th = [half_coef(smat_ref[p, t], tabs) for t in range(6)]
        tb = [1.0 / (th[t][0] + th[t + 1][0]) for t in range(5)]

        def cols(b, a, f):
            return b[24:120, f : f + 1], a[24:120, f : f + 1]

        for t in str_layers:
            update_layer(
                t, 3, lambda c, m: stringer(p, c, m), lambda c, m: str_prev(p, c, m), th[t][0], th[t][1], lambda m: tb[m],
                lambda c: None, lambda c: cols(before_ref, after_ref, (p * 3 + c) * 6 + t),
                None, cols(hb_ref, ha_ref, 36 + p * 6 + t),
                (lambda c: str_load(p, c)) if (t == 0 and str_load is not None) else None,
                lambda c, v: put_str(p, c, t, v),
            )


def first_body(
    stiff_ref, coef_ref, skin_ref, skin_prev_ref, mat_ref, str_ref, str_prev_ref, smat_ref,
    before_ref, after_ref, lefts_ref, rights_ref,
    skin1_ref, str1_ref, last_ref, first_ref, right_ref, left_ref,
):
    tabs = tables(stiff_ref, coef_ref)
    lane = iota((128, 128), 1)
    slane = iota((96, 128), 1)
    zero = jnp.zeros((128, 128), F32)
    right_ref[...] = zero
    left_ref[...] = zero
    last_ref[...] = jnp.zeros((120, 128), F32)
    first_ref[...] = jnp.zeros((120, 128), F32)

    def put_skin(c, l, value):
        skin1_ref[c, l] = value
        f = c * 6 + l
        last_ref[f : f + 1, :] = value[127:128, :]
        first_ref[f : f + 1, :] = value[0:1, :]
        right_ref[...] = jnp.where(lane == f, value[:, 127:128], right_ref[...])
        left_ref[...] = jnp.where(lane == f, value[:, 0:1], left_ref[...])

    def put_str(p, c, t, value):
        str1_ref[p, c, t - 1] = value
        f = (p * 3 + c) * 6 + t
        last_ref[24:120, :] = jnp.where(slane == f, value[:, 127:128], last_ref[24:120, :])
        first_ref[24:120, :] = jnp.where(slane == f, value[:, 0:1], first_ref[24:120, :])

    halos = (before_ref, after_ref, lefts_ref, rights_ref) * 2
    whole_step(
        tabs, mat_ref, smat_ref, lambda c, l: skin_ref[c, l], lambda c, l: skin_prev_ref[c, l],
        lambda p, c, t: str_ref[p, c, t], lambda p, c, t: str_prev_ref[p, c, t], halos,
        range(5), range(1, 6), None, None, put_skin, put_str,
    )


def second_body(
    stiff_ref, coef_ref, skin_ref, skin_prev_ref, mat_ref, str_ref, str_prev_ref, smat_ref,
    hb_ref, ha_ref, hl_ref, hr_ref, before_ref, after_ref, lefts_ref, rights_ref,
    skin_face_ref, str_face_ref, sload_ref, tload_ref, skin2_ref, str2_ref,
):
    tabs = tables(stiff_ref, coef_ref)
    halos = (before_ref, after_ref, lefts_ref, rights_ref, hb_ref, ha_ref, hl_ref, hr_ref)

    def put_skin(c, l, value):
        skin2_ref[c, l] = value

    def put_str(p, c, t, value):
        str2_ref[p, c, t] = value

    whole_step(
        tabs, mat_ref, smat_ref,
        lambda c, l: skin_face_ref[c] if l == 5 else skin_ref[c, l], lambda c, l: skin_prev_ref[c, l],
        lambda p, c, t: str_face_ref[p, c] if t == 0 else str_ref[p, c, t - 1],
        lambda p, c, t: str_prev_ref[p, c, t], halos, range(6), range(6),
        lambda c: sload_ref[c], lambda p, c: tload_ref[p, c], put_skin, put_str,
    )


def swap(values):
    return lax.all_to_all(values, "chord", split_axis=0, concat_axis=0, tiled=True)


def blocks(shape, at):
    return pl.BlockSpec(shape, lambda i: at)


def gather_call(ins):
    whole = lambda a: pl.BlockSpec(a.shape, lambda i, n=a.ndim: (0,) * n)
    specs = [pl.BlockSpec(memory_space=pltpu.SMEM)] * 2 + [whole(ins[2])]
    specs += [
        blocks((3, 2, 128, 128), (0, 2, 0, 0)),
        blocks((3, 1, 128, 128), (0, 5, 0, 0)),
        blocks((2, 128, 128), (2, 0, 0)),
        blocks((2, 3, 2, 96, 128), (0, 0, 0, 0, 0)),
        blocks((2, 3, 1, 96, 128), (0, 0, 0, 0, 0)),
        blocks((2, 2, 96, 128), (0, 0, 0, 0)),
    ] + [whole(a) for a in ins[9:]]
    outs = [(32, 512), (128, 128), (3, 128, 128), (128, 128), (96, 256), (3, 96, 256), (96, 256)]
    return pl.pallas_call(
        gather_body, grid=(1,), in_specs=specs,
        out_shape=[jax.ShapeDtypeStruct(s, F32) for s in outs],
        out_specs=[pl.BlockSpec(s, lambda i, n=len(s): (0,) * n) for s in outs],
        compiler_params=params(), name="gather",
        cost_estimate=pl.CostEstimate(flops=1000000000, bytes_accessed=2000000, transcendentals=0),
    )(*ins)


def load_call(ins):
    whole = lambda a: pl.BlockSpec(a.shape, lambda i, n=a.ndim: (0,) * n)
    specs = [whole(a) for a in ins[:8]]
    specs += [blocks((3, 1, 128, 128), (0, 5, 0, 0)), blocks((2, 3, 1, 96, 128), (0, 0, 0, 0, 0))]
    specs += [whole(a) for a in ins[10:]]
    outs = [(3, 128, 128), (3, 128, 128), (2, 3, 96, 128), (2, 3, 96, 128), (120, 128), (120, 128), (128, 128), (128, 128)]
    return pl.pallas_call(
        load_body, grid=(1,), in_specs=specs,
        out_shape=[jax.ShapeDtypeStruct(s, F32) for s in outs],
        out_specs=[pl.BlockSpec(s, lambda i, n=len(s): (0,) * n) for s in outs],
        compiler_params=params(), name="load",
        cost_estimate=pl.CostEstimate(flops=1000000000, bytes_accessed=2000000, transcendentals=0),
    )(*ins)


def shards(
    skin_now, skin_prev, skin_mat, stringer_now, stringer_prev, stringer_mat, owner_slot,
    rivet_span, rivet_chord, rivet_stringer, rivet_cell, rivet_stiff, mat_stiff, mat_coef,
):
    rivets = [a.reshape(1, -1) for a in (rivet_span, rivet_chord, rivet_stringer, rivet_cell, rivet_stiff)]
    sent, match = call(prep_body, [(32, 128), (128, 128)], rivets + [owner_slot.reshape(-1, 1)], "prep")
    rows = swap(sent)
    packs = call(
        halo_body, [(120, 128), (120, 128), (128, 128), (128, 128)],
        [mat_stiff, mat_coef, skin_now, skin_mat, stringer_now, stringer_mat], "halo", smem=(0, 1),
        flops=4000000, nbytes=4000000,
    )
    halos = exchange(*packs)
    mats = [mat_stiff, mat_coef]
    own = [skin_now, skin_prev, skin_mat, stringer_now, stringer_prev, stringer_mat]
    found, *kept = gather_call([*mats, rows, *own, *halos])
    given = swap(found)
    skin1, str1, *packs1 = call(
        first_body, [(3, 5, 128, 128), (2, 3, 5, 96, 128), (120, 128), (120, 128), (128, 128), (128, 128)],
        [*mats, *own, *halos], "first", smem=(0, 1), flops=20000000, nbytes=10000000,
    )
    (turned,) = call(bounce_body, [(32, 512)], [match, given], "bounce")
    posted = swap(turned)
    skin_face, sload, str_face, tload, *packs2 = load_call([rows, posted, *kept, skin_now, stringer_now, *packs1])
    halos1 = exchange(*packs2)
    return call(
        second_body, [(3, 6, 128, 128), (2, 3, 6, 96, 128)],
        [*mats, skin1, skin_now, skin_mat, str1, stringer_now, stringer_mat, *halos, *halos1, skin_face, str_face, sload, tload],
        "second", smem=(0, 1), flops=20000000, nbytes=10000000,
    )


def solution(mesh):
    placed = (
        P(None, None, "span", "chord"),
        P(None, None, "span", "chord"),
        P(None, "span", "chord"),
        P("chord", None, None, None, "span"),
        P("chord", None, None, None, "span"),
        P("chord", None, None, "span"),
        P(),
        P(("span", "chord")),
        P(("span", "chord")),
        P(("span", "chord")),
        P(("span", "chord")),
        P(("span", "chord")),
        P(),
        P(),
    )
    body = jax.shard_map(
        shards,
        mesh=mesh,
        in_specs=placed,
        out_specs=(P(None, None, "span", "chord"), P("chord", None, None, None, "span")),
        check_vma=False,
    )
    return lambda *args: tuple(body(*args))
```

```python
import jax
import jax.numpy as jnp
from jax import lax
from jax.experimental import pallas as pl
from jax.experimental.pallas import tpu as pltpu
from jax.sharding import PartitionSpec as P

F32 = jnp.float32
BF16 = jnp.bfloat16
NT = (((1,), (1,)), ((), ()))
TN = (((0,), (0,)), ((), ()))
FIELDS = 7


def iota(shape, dim):
    return lax.broadcasted_iota(jnp.int32, shape, dim)


def two_parts(values):
    high = values.astype(BF16)
    return high, (values - high.astype(F32)).astype(BF16)


def pick(mask, values):
    return jnp.where(mask, values, 0.0).astype(BF16)


def whole(shape):
    return pl.BlockSpec(tuple(shape), lambda i: (0,) * len(shape), pipeline_mode=pl.Buffered(1))


def call(body, outs, ins, name, smem=(), flops=0, nbytes=0, scratch=()):
    specs = [pl.BlockSpec(memory_space=pltpu.SMEM) if i in smem else whole(a.shape) for i, a in enumerate(ins)]
    return pl.pallas_call(
        body,
        grid=(1,),
        out_shape=[jax.ShapeDtypeStruct(s, F32) for s in outs],
        in_specs=specs,
        out_specs=[whole(s) for s in outs],
        scratch_shapes=[pltpu.VMEM(s, F32) for s in scratch],
        compiler_params=pltpu.CompilerParams(vmem_limit_bytes=56 * 1024 * 1024),
        cost_estimate=pl.CostEstimate(flops=flops, bytes_accessed=nbytes, transcendentals=0),
        name=name,
    )(*ins)


def tables(stiff_ref, coef_ref):
    half = [0.5 / jnp.full((1, 128), stiff_ref[m], F32) for m in range(8)]
    return half, [coef_ref[m] for m in range(8)]


def half_of(mat, tabs):
    out = jnp.broadcast_to(tabs[0][0], mat.shape)
    for m in range(1, 8):
        out = jnp.where(mat == m, tabs[0][m], out)
    return out


def half_coef(mat, tabs):
    half = jnp.broadcast_to(tabs[0][0], mat.shape)
    coef = jnp.full(mat.shape, tabs[1][0], F32)
    for m in range(1, 8):
        same = mat == m
        half = jnp.where(same, tabs[0][m], half)
        coef = jnp.where(same, tabs[1][m], coef)
    return half, coef


CHUNK = 32


def joined(before, after):
    lane = iota(before.shape, 1)
    return jnp.where((lane & 1) == 1, pltpu.roll(before, 1, 1), pltpu.roll(after, 127, 1))


def with_columns(columns, cells, field):
    lane = iota(cells.shape, 1)
    return jnp.where((lane >> 1) == field, pltpu.roll(cells, 2 * field + 1, 1), columns)


def row_neighbours(get, r0, total, ends):
    cells = get(r0, CHUNK)
    row = iota(cells.shape, 0)
    if r0 > 0:
        above = get(r0 - 1, CHUNK)
    else:
        above = pltpu.roll(cells, 1, 0)
        if ends is not None:
            above = jnp.where(row == 0, ends[0], above)
    if r0 + CHUNK < total:
        below = get(r0 + 1, CHUNK)
    else:
        below = pltpu.roll(cells, CHUNK - 1, 0)
        if ends is not None:
            below = jnp.where(row == CHUNK - 1, ends[1], below)
    return cells, above, below


def lane_neighbours(cells, edge, field):
    lane = iota(cells.shape, 1)
    turned = pltpu.roll(edge, (127 - 2 * field) % 128, 1)
    before = jnp.where(lane == 0, turned, pltpu.roll(cells, 1, 1))
    after = jnp.where(lane == 127, turned, pltpu.roll(cells, 127, 1))
    return before, after


def safe_bond(half, beside):
    return jnp.where(beside > 0.0, 1.0 / (half + beside), 0.0)


def layer_bonds(get, total, ends, edge, field, down, across, left):
    for r0 in range(0, total, CHUNK):
        half, _, below = row_neighbours(get, r0, total, ends)
        bond = safe_bond(half, below)
        if ends is None and r0 + CHUNK == total:
            bond = jnp.where(iota(half.shape, 0) == CHUNK - 1, 0.0, bond)
        down[8 + r0 : 8 + r0 + CHUNK, :] = bond
        if r0 == 0:
            down[7:8, :] = jnp.zeros((1, 128), F32) if ends is None else safe_bond(half[0:1], ends[0])
        before, after = lane_neighbours(half, edge[r0 : r0 + CHUNK, :], field)
        left[r0 : r0 + CHUNK, :] = safe_bond(half, before)
        across[r0 : r0 + CHUNK, :] = safe_bond(half, after)


def chunk_step(now, prev, total, r0, layer, comps, bonds, edge, fields, ends, extra, put):
    down, across, left, thick, coef = bonds
    sl = pl.ds(r0, CHUNK)
    up = down(layer)[pl.ds(7 + r0, CHUNK), :]
    dn = down(layer)[pl.ds(8 + r0, CHUNK), :]
    ac, al, co = across(layer)[sl, :], left(layer)[sl, :], coef(layer)[sl, :]
    for c in range(comps):
        cells, above, below = row_neighbours(now(c, layer), r0, total, None if ends is None else ends(c))
        before, after = lane_neighbours(cells, edge[sl, :], fields(c))
        pull = dn * (below - cells) + up * (above - cells)
        pull = pull + (ac * (after - cells) + al * (before - cells))
        if layer < 5:
            pull = pull + thick(layer)[sl, :] * (now(c, layer + 1)(r0, CHUNK) - cells)
        if layer > 0:
            pull = pull + thick(layer - 1)[sl, :] * (now(c, layer - 1)(r0, CHUNK) - cells)
        if extra is not None:
            pull = pull + extra(c)
        put(c, 2.0 * cells - prev(c, layer)(r0, CHUNK) + co * pull)


def rows_of(ref, *index):
    view = ref.at[index]
    return lambda lo, n: view[pl.ds(lo, n), :]


def ends_of(before, after, index):
    return before[index : index + 1, :], after[index : index + 1, :]


def prep_body(span_ref, chord_ref, stringer_ref, cell_ref, stiff_ref, owner_ref, out_ref, match_ref):
    def row_of(ref):
        return ref[...].reshape(1, -1)

    span, chord, stringer = row_of(span_ref), row_of(chord_ref), row_of(stringer_ref)
    cell, stiff = row_of(cell_ref), row_of(stiff_ref)
    count = span.shape[1]
    chunks = count // 128
    same = iota((48, count), 0) == stringer
    diagonal = iota((48, 48), 0) == iota((48, 48), 1)
    owner = jnp.sum(jnp.where(diagonal, owner_ref[...], 0).astype(F32), axis=1, keepdims=True).astype(jnp.int32)
    slot = jnp.sum(jnp.where(same, owner, 0).astype(F32), axis=0, keepdims=True).astype(jnp.int32)
    foot = (chord - (((2 * cell) * 171) >> 9)) >> 6
    foot_of = jnp.max(jnp.where(same, foot, 0).astype(F32), axis=1, keepdims=True).astype(jnp.int32)
    slots = iota((48, 64), 1)
    slot_hot = (slots == (owner & 1) * 32 + (owner >> 1)).astype(F32).astype(BF16)
    foot_hot = (slots == (foot_of & 1) * 32 + (foot_of >> 1)).astype(F32).astype(BF16)
    match_ref[0:64, 0:64] = lax.dot_general(foot_hot, slot_hot, TN, preferred_element_type=F32)
    match_ref[64:128, 0:64] = lax.dot_general(slot_hot, foot_hot, TN, preferred_element_type=F32)
    one = same.astype(F32)
    lower = (iota((128, 128), 0) < iota((128, 128), 1)).astype(F32).astype(BF16)
    both = jnp.concatenate([lower, jnp.ones((128, 128), BF16)], axis=1)
    offset = jnp.zeros((48, 128), F32)
    ranks = []
    for k in range(chunks):
        part = one[:, k * 128 : (k + 1) * 128]
        ahead = jnp.dot(part.astype(BF16), both, preferred_element_type=F32)
        ranks.append(jnp.sum(part * (ahead[:, :128] + offset), axis=0, keepdims=True))
        offset = offset + ahead[:, 128:]
    rank = jnp.concatenate(ranks, axis=1).astype(jnp.int32)
    place = iota((128, count), 0)
    place = place == jnp.where(
        place < 64, (slot & 1) * 32 + (slot >> 1), 64 + (foot & 1) * 32 + (foot >> 1)
    )
    place = place.astype(F32).astype(BF16)
    order = iota((16, count), 0) == rank
    high = stiff.astype(BF16).astype(F32)
    rest = stiff - high
    middle = rest.astype(BF16).astype(F32)
    fields = [cell.astype(F32), (span & 127).astype(F32), (chord & 127).astype(F32), high, middle, rest - middle]
    rows = jnp.concatenate([pick(order, f) for f in fields], axis=0)
    got = lax.dot_general(place, rows, NT, preferred_element_type=F32)
    for side in range(2):
        index, weight = [], []
        for p in range(2):
            part = got[side * 64 + p * 32 : side * 64 + p * 32 + 32]
            where_, across = part[:, 0:16], part[:, 16:32]
            if side == 1:
                where_, across = part[:, 16:32], part[:, 32:48]
            index.append(where_ * 128.0 + across)
            weight.append(part[:, 48:64] + part[:, 64:80] + part[:, 80:96])
        out_ref[:, side * 64 : side * 64 + 64] = jnp.concatenate(index + weight, axis=1)


def ends_exist():
    span, chord = lax.axis_index("span"), lax.axis_index("chord")
    yes = lambda cond: jnp.where(cond, 1.0, 0.0).astype(F32)
    return (
        yes(span > 0), yes(span < lax.axis_size("span") - 1),
        yes(chord > 0), yes(chord < lax.axis_size("chord") - 1),
    )


def pack_skin(columns, get, layers, r0, first_ref, last_ref):
    for l in layers:
        for c in range(3):
            f = c * 6 + l
            cells = get(c, l)
            columns = with_columns(columns, cells, f)
            if r0 == 0:
                first_ref[f : f + 1, :] = cells[0:1]
            if r0 == 128 - CHUNK:
                last_ref[f : f + 1, :] = cells[CHUNK - 1 : CHUNK]
    return columns


def pack_str(columns, get, layers):
    for p in range(2):
        for t in layers:
            for c in range(3):
                columns = with_columns(columns, get(p, c, t), (p * 3 + c) * 6 + t)
    return columns


def halo_body(stiff_ref, coef_ref, skin_ref, mat_ref, str_ref, smat_ref, after_ref, last_ref, first_ref, side_ref):
    tabs = tables(stiff_ref, coef_ref)
    at_prev, at_next, at_left, at_right = ends_exist()
    lane = iota((CHUNK, 128), 1)
    side_keep = jnp.where((lane & 1) == 0, at_right, at_left)
    span_keep = jnp.where((lane & 1) == 0, at_next, at_prev)
    for r0 in range(0, 128, CHUNK):
        columns = jnp.zeros((CHUNK, 128), F32)
        for l in range(6):
            half = half_of(mat_ref[l, pl.ds(r0, CHUNK), :], tabs)
            columns = with_columns(columns, half, 18 + l)
            if r0 == 0:
                first_ref[18 + l : 19 + l, :] = half[0:1] * at_prev
            if r0 == 128 - CHUNK:
                last_ref[18 + l : 19 + l, :] = half[CHUNK - 1 : CHUNK] * at_next
        columns = columns * side_keep
        side_ref[pl.ds(r0, CHUNK), :] = pack_skin(
            columns, lambda c, l: skin_ref[c, l, pl.ds(r0, CHUNK), :], range(6), r0, first_ref, last_ref
        )
    for r0 in range(0, 96, CHUNK):
        columns = jnp.zeros((CHUNK, 128), F32)
        for p in range(2):
            for t in range(6):
                half = half_of(smat_ref[p, t, pl.ds(r0, CHUNK), :], tabs)
                columns = with_columns(columns, half, 36 + p * 6 + t)
        columns = columns * span_keep
        columns = pack_str(columns, lambda p, c, t: str_ref[p, c, t, pl.ds(r0, CHUNK), :], range(6))
        last_ref[pl.ds(24 + r0, CHUNK), :] = columns
        first_ref[pl.ds(24 + r0, CHUNK), :] = columns


def exchange(last, first, side):
    def ring(axis):
        count = lax.axis_size(axis)
        return [(i, (i + 1) % count) for i in range(count)]

    back = lambda pairs: [(b, a) for a, b in pairs]
    before = lax.ppermute(last, "span", ring("span"))
    after = lax.ppermute(first, "span", back(ring("span")))
    lefts = lax.ppermute(side, "chord", ring("chord"))
    rights = lax.ppermute(side, "chord", back(ring("chord")))
    return before, after, lefts, rights


def row_lists(index):
    return jnp.concatenate([index[q * 8 : q * 8 + 8, :] for q in range(4)], axis=1)


def one_row(values):
    return jnp.concatenate([values[a : a + 1, :] for a in range(8)], axis=1)


def hots(rows_ref):
    text = one_row(row_lists(rows_ref[:, 0:32])).astype(jnp.int32)
    tk = one_row(row_lists(rows_ref[:, 32:64]))
    sext = one_row(row_lists(rows_ref[:, 64:96])).astype(jnp.int32)
    sk = one_row(row_lists(rows_ref[:, 96:128]))
    slot = ((iota((1, 1024), 1) >> 4) & 1) * 128
    t_row = iota((96, 1024), 0) == (text >> 7)
    t_lane = (iota((256, 1024), 0) == (text & 127) + slot).astype(F32).astype(BF16)
    s_row = iota((128, 1024), 0) == (sext >> 7)
    s_lane = (iota((128, 1024), 0) == (sext & 127)).astype(F32).astype(BF16)
    return (t_row, t_lane, tk), (s_row, s_lane, sk)


def spread(row_mask, lane_hot, values):
    high, low = two_parts(values)
    left = jnp.concatenate([pick(row_mask, high.astype(F32)), pick(row_mask, low.astype(F32))], axis=1)
    right = jnp.concatenate([lane_hot, lane_hot], axis=1)
    return lax.dot_general(left, right, NT, preferred_element_type=F32)


def fetch(row_mask, lane_hot2, cells):
    high, low = two_parts(cells)
    wide = jnp.dot(jnp.concatenate([high, low], axis=1), lane_hot2, preferred_element_type=F32)
    return jnp.sum(jnp.where(row_mask, wide, 0.0), axis=0, keepdims=True)


def as_lanes(row):
    return jnp.concatenate([row[:, a * 128 : (a + 1) * 128] for a in range(8)], axis=0)


def gather_body(
    stiff_ref, coef_ref, rows_ref, skin_ref, skin_prev_ref, mat_ref, str_ref, str_prev_ref, smat_ref,
    before_ref, after_ref, lefts_ref, rights_ref,
    out_ref, ks_ref, ps_ref, cs_ref, kt_ref, pt_ref, ct_ref,
    half_ref, down_ref, across_ref, left_ref, thick_ref, edge_ref, tedge_ref, co_ref,
):
    tabs = tables(stiff_ref, coef_ref)
    (t_row, t_lane, tk), (s_row, s_lane, sk) = hots(rows_ref)
    ks_ref[...] = spread(s_row, s_lane, sk)
    kt_ref[...] = spread(t_row, t_lane, tk)
    edge_ref[...] = joined(lefts_ref[...], rights_ref[...])
    tedge_ref[...] = joined(before_ref[24:120, :], after_ref[24:120, :])
    bonds = (lambda l: down_ref, lambda l: across_ref, lambda l: left_ref, lambda l: thick_ref, lambda l: co_ref)

    def prepare(total, own, other, ends, edge, field):
        for r0 in range(0, total, CHUNK):
            sl = pl.ds(r0, CHUNK)
            half, coef = half_coef(own[sl, :], tabs)
            half_ref[sl, :] = half
            co_ref[sl, :] = coef
            thick_ref[sl, :] = 1.0 / (half + half_of(other[sl, :], tabs))
        layer_bonds(lambda lo, n: half_ref[pl.ds(lo, n), :], total, ends, edge, field, down_ref, across_ref, left_ref)

    prepare(128, mat_ref.at[5], mat_ref.at[4], ends_of(before_ref, after_ref, 23), edge_ref, 23)
    cs_ref[...] = co_ref[...]
    for r0 in range(0, 128, CHUNK):
        sl = pl.ds(r0, CHUNK)

        def put(c, value):
            ps_ref[c, sl, :] = value - cs_ref[sl, :] * ks_ref[sl, :] * skin_ref[c, 5, sl, :]

        chunk_step(
            lambda c, l: rows_of(skin_ref, c, l), lambda c, l: rows_of(skin_prev_ref, c, l), 128, r0, 5, 3, bonds,
            edge_ref, lambda c: c * 6 + 5, lambda c: ends_of(before_ref, after_ref, c * 6 + 5), None, put,
        )
    for p in range(2):
        prepare(96, smat_ref.at[p, 0], smat_ref.at[p, 1], None, tedge_ref, 36 + p * 6)
        lanes = pl.ds(p * 128, 128)
        ct_ref[:, p * 128 : p * 128 + 128] = co_ref[0:96, :]
        for r0 in range(0, 96, CHUNK):
            sl = pl.ds(r0, CHUNK)

            def put(c, value):
                pt_ref[c, sl, lanes] = value - ct_ref[sl, lanes] * kt_ref[sl, lanes] * str_ref[p, c, 0, sl, :]

            chunk_step(
                lambda c, l: rows_of(str_ref, p, c, l), lambda c, l: rows_of(str_prev_ref, p, c, l), 96, r0, 0, 3, bonds,
                tedge_ref, lambda c: (p * 3 + c) * 6, None, None, put,
            )
    t_fields = [jnp.concatenate([str_ref[0, c, 0], str_ref[1, c, 0]], axis=1) for c in range(3)]
    t_fields += [pt_ref[c] for c in range(3)] + [ct_ref[...] * kt_ref[...]]
    s_fields = [skin_ref[c, 5] for c in range(3)] + [ps_ref[c] for c in range(3)] + [cs_ref[...]]
    t_two = jnp.concatenate([t_lane, t_lane], axis=0)
    s_two = jnp.concatenate([s_lane, s_lane], axis=0)
    got = [as_lanes(fetch(t_row, t_two, f)) for f in t_fields]
    got += [as_lanes(fetch(s_row, s_two, f)) for f in s_fields]
    pad = jnp.zeros((8, 128), F32)
    got += [pad, pad]
    for j in range(4):
        part = [
            jnp.concatenate([g[:, q * 32 : q * 32 + 32] for g in got[4 * j : 4 * j + 4]], axis=1) for q in range(4)
        ]
        out_ref[pl.ds(j, 32, stride=4), :] = jnp.concatenate(part, axis=0)


def bounce_body(match_ref, got_ref, after_ref, out_ref):
    got = jnp.concatenate([got_ref[pl.ds(j, 32, stride=4), :] for j in range(4)], axis=1)
    lane = iota(got.shape, 1)
    zero = (lane & 16) == 0

    def turned(base):
        def part(to, frm):
            m = match_ref[base + to * 32 : base + to * 32 + 32, frm * 32 : frm * 32 + 32]
            return jnp.dot(m, got, preferred_element_type=F32, precision=lax.Precision.HIGHEST)

        a = part(0, 0) + pltpu.roll(part(0, 1), 512 - 16, 1)
        b = part(1, 1) + pltpu.roll(part(1, 0), 16, 1)
        return jnp.where(zero, a, b)

    new = jnp.where(lane < FIELDS * 32, turned(0), turned(64))
    for j in range(4):
        out_ref[pl.ds(j, 32, stride=4), :] = new[:, j * 128 : j * 128 + 128]


def load_body(
    rows_ref, posted_ref, ks_ref, ps_ref, cs_ref, kt_ref, pt_ref, ct_ref, skin_ref, str_ref,
    last_in, first_in, side_in,
    skin1_ref, sload_ref, str1_ref, tload_ref, last_ref, first_ref, side_ref,
):
    (t_row, t_lane, tk), (s_row, s_lane, sk) = hots(rows_ref)
    posted = [posted_ref[pl.ds(j, 32, stride=4), :] for j in range(4)]

    def sums(side, row_mask, lane_hot, weight, f):
        g = side * FIELDS + f
        at = g % 4 * 32
        return spread(row_mask, lane_hot, weight * one_row(row_lists(posted[g // 4][:, at : at + 32])))

    last_ref[...] = last_in[...]
    first_ref[...] = first_in[...]
    side = side_in[...]
    ks, cs = ks_ref[...], cs_ref[...]
    qs = sums(0, s_row, s_lane, sk, 6)
    for c in range(3):
        now = skin_ref[c, 5]
        new = ps_ref[c] + cs * sums(0, s_row, s_lane, sk, c)
        skin1_ref[c] = new
        sload_ref[c] = sums(0, s_row, s_lane, sk, 3 + c) + qs * now - ks * new
        f = c * 6 + 5
        last_ref[f : f + 1, :] = new[127:128, :]
        first_ref[f : f + 1, :] = new[0:1, :]
        side = with_columns(side, new, f)
    side_ref[...] = side
    kt, ct = kt_ref[...], ct_ref[...]
    qt = sums(1, t_row, t_lane, tk, 6)
    third = iota((96, 256), 0) % 3
    columns = last_in[24:120, :]
    for c in range(3):
        now = jnp.concatenate([str_ref[0, c, 0], str_ref[1, c, 0]], axis=1)
        own = kt * now
        pair = jnp.where(third == 0, pltpu.roll(own, 95, 0), jnp.where(third == 1, pltpu.roll(own, 1, 0), 0.0))
        new = pt_ref[c] + ct * sums(1, t_row, t_lane, tk, c)
        load = sums(1, t_row, t_lane, tk, 3 + c) + qt * (own + pair) - kt * new
        for p in range(2):
            str1_ref[p, c] = new[:, p * 128 : p * 128 + 128]
            tload_ref[p, c] = load[:, p * 128 : p * 128 + 128]
            columns = with_columns(columns, new[:, p * 128 : p * 128 + 128], (p * 3 + c) * 6)
    last_ref[24:120, :] = columns
    first_ref[24:120, :] = columns


def bonds_body(
    stiff_ref, coef_ref, mat_ref, smat_ref, before_ref, after_ref, lefts_ref, rights_ref, later_ref,
    sd_ref, sa_ref, sl_ref, st_ref, sc_ref, td_ref, ta_ref, tl_ref, tt_ref, tc_ref,
    token_ref, sh_ref, th_ref, edge_ref, tedge_ref,
):
    token_ref[...] = jnp.zeros((8, 128), F32)
    tabs = tables(stiff_ref, coef_ref)
    edge_ref[...] = joined(lefts_ref[...], rights_ref[...])
    tedge_ref[...] = joined(before_ref[24:120, :], after_ref[24:120, :])
    for r0 in range(0, 128, CHUNK):
        sl = pl.ds(r0, CHUNK)
        for l in range(6):
            half, coef = half_coef(mat_ref[l, sl, :], tabs)
            if l > 0:
                st_ref[l - 1, sl, :] = 1.0 / (half + sh_ref[l - 1, sl, :])
            sh_ref[l, sl, :] = half
            sc_ref[l, sl, :] = coef
    for l in range(6):
        layer_bonds(
            rows_of(sh_ref, l), 128, ends_of(before_ref, after_ref, 18 + l), edge_ref, 18 + l,
            sd_ref.at[l], sa_ref.at[l], sl_ref.at[l],
        )
    for p in range(2):
        for r0 in range(0, 96, CHUNK):
            sl = pl.ds(r0, CHUNK)
            for t in range(6):
                half, coef = half_coef(smat_ref[p, t, sl, :], tabs)
                if t > 0:
                    tt_ref[p, t - 1, sl, :] = 1.0 / (half + th_ref[t - 1, sl, :])
                th_ref[t, sl, :] = half
                tc_ref[p, t, sl, :] = coef
        for t in range(6):
            layer_bonds(
                rows_of(th_ref, t), 96, None, tedge_ref, 36 + p * 6 + t, td_ref.at[p, t], ta_ref.at[p, t], tl_ref.at[p, t]
            )


def skin_chunks(now, prev, bonds, edge_ref, before_ref, after_ref, layers, extra, put):
    for r0 in range(0, 128, CHUNK):
        for l in layers:
            chunk_step(
                now, prev, 128, r0, l, 3, bonds, edge_ref, lambda c: c * 6 + l,
                lambda c: ends_of(before_ref, after_ref, c * 6 + l),
                (lambda c: extra(c, r0)) if l == 5 and extra is not None else None, lambda c, v: put(c, l, r0, v),
            )


def str_chunks(now, prev, bonds, edge_ref, layers, extra, put):
    for r0 in range(0, 96, CHUNK):
        for p in range(2):
            for t in layers:
                chunk_step(
                    lambda c, m: now(p, c, m), lambda c, m: prev(p, c, m), 96, r0, t, 3, bonds(p), edge_ref,
                    lambda c: (p * 3 + c) * 6 + t, None,
                    (lambda c: extra(p, c, r0)) if t == 0 and extra is not None else None,
                    lambda c, v: put(p, c, t, r0, v),
                )


def at_layers(*refs):
    return tuple((lambda l, ref=ref: ref.at[l]) for ref in refs)


def first_body(
    skin_ref, skin_prev_ref, str_ref, str_prev_ref, before_ref, after_ref, lefts_ref, rights_ref,
    sd_ref, sa_ref, sl_ref, st_ref, sc_ref, td_ref, ta_ref, tl_ref, tt_ref, tc_ref, later_ref,
    skin1_ref, str1_ref, last_ref, first_ref, side_ref,
    edge_ref, tedge_ref,
):
    edge_ref[...] = joined(lefts_ref[...], rights_ref[...])
    tedge_ref[...] = joined(before_ref[24:120, :], after_ref[24:120, :])
    last_ref[0:24, :] = jnp.zeros((24, 128), F32)
    first_ref[0:24, :] = jnp.zeros((24, 128), F32)

    def put_skin(c, l, r0, value):
        skin1_ref[c, l, pl.ds(r0, CHUNK), :] = value

    def put_str(p, c, t, r0, value):
        str1_ref[p, c, t - 1, pl.ds(r0, CHUNK), :] = value

    skin_chunks(
        lambda c, l: rows_of(skin_ref, c, l), lambda c, l: rows_of(skin_prev_ref, c, l),
        at_layers(sd_ref, sa_ref, sl_ref, st_ref, sc_ref), edge_ref, before_ref, after_ref, range(5), None, put_skin,
    )
    str_chunks(
        lambda p, c, t: rows_of(str_ref, p, c, t), lambda p, c, t: rows_of(str_prev_ref, p, c, t),
        lambda p: at_layers(*(r.at[p] for r in (td_ref, ta_ref, tl_ref, tt_ref, tc_ref))), tedge_ref, range(1, 6), None,
        put_str,
    )
    for r0 in range(0, 128, CHUNK):
        side_ref[pl.ds(r0, CHUNK), :] = pack_skin(
            jnp.zeros((CHUNK, 128), F32), lambda c, l: skin1_ref[c, l, pl.ds(r0, CHUNK), :], range(5), r0, first_ref, last_ref
        )
    for r0 in range(0, 96, CHUNK):
        columns = pack_str(
            jnp.zeros((CHUNK, 128), F32), lambda p, c, t: str1_ref[p, c, t - 1, pl.ds(r0, CHUNK), :], range(1, 6)
        )
        last_ref[pl.ds(24 + r0, CHUNK), :] = columns
        first_ref[pl.ds(24 + r0, CHUNK), :] = columns


def second_body(
    skin_ref, skin_prev_ref, str_ref, str_prev_ref, before_ref, after_ref, lefts_ref, rights_ref,
    sd_ref, sa_ref, sl_ref, st_ref, sc_ref, td_ref, ta_ref, tl_ref, tt_ref, tc_ref,
    skin_face_ref, str_face_ref, sload_ref, tload_ref, skin2_ref, str2_ref,
    edge_ref, tedge_ref,
):
    edge_ref[...] = joined(lefts_ref[...], rights_ref[...])
    tedge_ref[...] = joined(before_ref[24:120, :], after_ref[24:120, :])

    def put_skin(c, l, r0, value):
        skin2_ref[c, l, pl.ds(r0, CHUNK), :] = value

    def put_str(p, c, t, r0, value):
        str2_ref[p, c, t, pl.ds(r0, CHUNK), :] = value

    skin_chunks(
        lambda c, l: rows_of(skin_face_ref, c) if l == 5 else rows_of(skin_ref, c, l),
        lambda c, l: rows_of(skin_prev_ref, c, l),
        at_layers(sd_ref, sa_ref, sl_ref, st_ref, sc_ref), edge_ref, before_ref, after_ref, range(6),
        lambda c, r0: sload_ref[c, pl.ds(r0, CHUNK), :], put_skin,
    )
    str_chunks(
        lambda p, c, t: rows_of(str_face_ref, p, c) if t == 0 else rows_of(str_ref, p, c, t - 1),
        lambda p, c, t: rows_of(str_prev_ref, p, c, t),
        lambda p: at_layers(*(r.at[p] for r in (td_ref, ta_ref, tl_ref, tt_ref, tc_ref))), tedge_ref, range(6),
        lambda p, c, r0: tload_ref[p, c, pl.ds(r0, CHUNK), :], put_str,
    )


def swap(values):
    peers = lax.axis_size("chord")
    moved = lax.all_to_all(values.reshape(peers, -1, 128), "chord", split_axis=0, concat_axis=0, tiled=True)
    return moved.reshape(values.shape)


def shards(
    skin_now, skin_prev, skin_mat, stringer_now, stringer_prev, stringer_mat, owner_slot,
    rivet_span, rivet_chord, rivet_stringer, rivet_cell, rivet_stiff, mat_stiff, mat_coef,
):
    rivets = [rivet_span, rivet_chord, rivet_stringer, rivet_cell, rivet_stiff]
    sent, match = call(prep_body, [(32, 128), (128, 128)], rivets + [owner_slot.reshape(1, -1)], "prep")
    rows = swap(sent)
    mats = [mat_stiff, mat_coef]
    column = [(120, 128), (120, 128), (128, 128)]
    packs = call(
        halo_body, column, [*mats, skin_now, skin_mat, stringer_now, stringer_mat, match], "halo", smem=(0, 1),
        flops=4000000, nbytes=4000000,
    )
    halos = exchange(*packs)
    edges = [(128, 128), (96, 128)]
    found, *kept = call(
        gather_body, [(128, 128), (128, 128), (3, 128, 128), (128, 128), (96, 256), (3, 96, 256), (96, 256)],
        [*mats, rows, skin_now, skin_prev, skin_mat, stringer_now, stringer_prev, stringer_mat, *halos], "gather",
        smem=(0, 1), flops=1000000000, nbytes=2000000,
        scratch=[(128, 128), (136, 128), (128, 128), (128, 128), (128, 128), *edges, (128, 128)],
    )
    given = swap(found)
    bonds = call(
        bonds_body,
        [(6, 136, 128), *[(6, 128, 128)] * 4, (2, 6, 104, 128), *[(2, 6, 96, 128)] * 4, (8, 128)],
        [*mats, skin_mat, stringer_mat, *halos, found], "bonds", smem=(0, 1), flops=10000000, nbytes=8000000,
        scratch=[(6, 128, 128), (6, 96, 128), *edges],
    )
    (turned,) = call(bounce_body, [(128, 128)], [match, given, bonds[-1]], "bounce")
    posted = swap(turned)
    skin1, str1, *packs1 = call(
        first_body, [(3, 5, 128, 128), (2, 3, 5, 96, 128), *column],
        [skin_now, skin_prev, stringer_now, stringer_prev, *halos, *bonds[:-1], turned], "first",
        flops=20000000, nbytes=10000000, scratch=edges,
    )
    skin_face, sload, str_face, tload, *packs2 = call(
        load_body, [(3, 128, 128), (3, 128, 128), (2, 3, 96, 128), (2, 3, 96, 128), *column],
        [rows, posted, *kept, skin_now, stringer_now, *packs1], "load", flops=1000000000, nbytes=2000000,
    )
    halos1 = exchange(*packs2)
    return call(
        second_body, [(3, 6, 128, 128), (2, 3, 6, 96, 128)],
        [skin1, skin_now, str1, stringer_now, *halos1, *bonds[:-1], skin_face, str_face, sload, tload], "second",
        flops=20000000, nbytes=10000000, scratch=edges,
    )


def solution(mesh):
    placed = (
        P(None, None, "span", "chord"),
        P(None, None, "span", "chord"),
        P(None, "span", "chord"),
        P("chord", None, None, None, "span"),
        P("chord", None, None, None, "span"),
        P("chord", None, None, "span"),
        P(),
        P(("span", "chord")),
        P(("span", "chord")),
        P(("span", "chord")),
        P(("span", "chord")),
        P(("span", "chord")),
        P(),
        P(),
    )
    body = jax.shard_map(
        shards,
        mesh=mesh,
        in_specs=placed,
        out_specs=(P(None, None, "span", "chord"), P("chord", None, None, None, "span")),
        check_vma=False,
    )
    return lambda *args: tuple(body(*args))
```

```python
import jax
import jax.numpy as jnp
from jax import lax
from jax.experimental import pallas as pl
from jax.experimental.pallas import tpu as pltpu
from jax.sharding import PartitionSpec as P

F32 = jnp.float32
BF16 = jnp.bfloat16
NT = (((1,), (1,)), ((), ()))
TN = (((0,), (0,)), ((), ()))
FIELDS = 7


def iota(shape, dim):
    return lax.broadcasted_iota(jnp.int32, shape, dim)


def two_parts(values):
    high = values.astype(BF16)
    return high, (values - high.astype(F32)).astype(BF16)


def pick(mask, values):
    return jnp.where(mask, values, 0.0).astype(BF16)


def whole(shape):
    return pl.BlockSpec(tuple(shape), lambda i: (0,) * len(shape), pipeline_mode=pl.Buffered(1))


def call(body, outs, ins, name, smem=(), far=(), fast=(), views=None, far_outs=(), flops=0, nbytes=0, scratch=(), sems=0, limit=56):
    views = views or {}

    def spec(i, a):
        if i in smem:
            return pl.BlockSpec(memory_space=pltpu.SMEM)
        if i in far:
            return pl.BlockSpec(memory_space=pl.ANY)
        if i in fast:
            return pl.BlockSpec(memory_space=pltpu.VMEM)
        if i in views:
            shape, at = views[i]
            return pl.BlockSpec(shape, lambda g: at)
        return whole(a.shape)

    return pl.pallas_call(
        body,
        grid=(1,),
        out_shape=[jax.ShapeDtypeStruct(s, F32) for s in outs],
        in_specs=[spec(i, a) for i, a in enumerate(ins)],
        out_specs=[pl.BlockSpec(memory_space=pl.ANY) if i in far_outs else whole(s) for i, s in enumerate(outs)],
        scratch_shapes=[pltpu.VMEM(s, t) for s, t in scratch] + ([pltpu.SemaphoreType.DMA((sems,))] if sems else []),
        compiler_params=pltpu.CompilerParams(vmem_limit_bytes=limit * 1024 * 1024),
        cost_estimate=pl.CostEstimate(flops=flops, bytes_accessed=nbytes, transcendentals=0),
        name=name,
    )(*ins)


def near(arrays):
    return [(a.shape, a.dtype) for a in arrays]


def floats(*shapes):
    return [(s, F32) for s in shapes]


def copies(sources, targets, sems, at=0):
    return [pltpu.make_async_copy(s, t, sems.at[at + i]) for i, (s, t) in enumerate(zip(sources, targets))]


def start(moves):
    for move in moves:
        move.start()


def finish(moves):
    for move in moves:
        move.wait()


def tables(stiff_ref, coef_ref):
    half = [0.5 / jnp.full((1, 128), stiff_ref[m], F32) for m in range(8)]
    return half, [coef_ref[m] for m in range(8)]


def half_of(mat, tabs):
    out = jnp.broadcast_to(tabs[0][0], mat.shape)
    for m in range(1, 8):
        out = jnp.where(mat == m, tabs[0][m], out)
    return out


def half_coef(mat, tabs):
    half = jnp.broadcast_to(tabs[0][0], mat.shape)
    coef = jnp.full(mat.shape, tabs[1][0], F32)
    for m in range(1, 8):
        same = mat == m
        half = jnp.where(same, tabs[0][m], half)
        coef = jnp.where(same, tabs[1][m], coef)
    return half, coef


CHUNK = 32


def joined(before, after):
    lane = iota(before.shape, 1)
    return jnp.where((lane & 1) == 1, pltpu.roll(before, 1, 1), pltpu.roll(after, 127, 1))


def with_columns(columns, cells, field):
    lane = iota(cells.shape, 1)
    return jnp.where((lane >> 1) == field, pltpu.roll(cells, 2 * field + 1, 1), columns)


def row_neighbours(get, r0, total, ends):
    cells = get(r0, CHUNK)
    row = iota(cells.shape, 0)
    if r0 > 0:
        above = get(r0 - 1, CHUNK)
    else:
        above = pltpu.roll(cells, 1, 0)
        if ends is not None:
            above = jnp.where(row == 0, ends[0], above)
    if r0 + CHUNK < total:
        below = get(r0 + 1, CHUNK)
    else:
        below = pltpu.roll(cells, CHUNK - 1, 0)
        if ends is not None:
            below = jnp.where(row == CHUNK - 1, ends[1], below)
    return cells, above, below


def lane_neighbours(cells, edge, field):
    lane = iota(cells.shape, 1)
    turned = pltpu.roll(edge, (127 - 2 * field) % 128, 1)
    before = jnp.where(lane == 0, turned, pltpu.roll(cells, 1, 1))
    after = jnp.where(lane == 127, turned, pltpu.roll(cells, 127, 1))
    return before, after


def safe_bond(half, beside):
    return jnp.where(beside > 0.0, 1.0 / (half + beside), 0.0)


def layer_bonds(get, total, ends, edge, field, down, across, left):
    for r0 in range(0, total, CHUNK):
        half, _, below = row_neighbours(get, r0, total, ends)
        bond = safe_bond(half, below)
        if ends is None and r0 + CHUNK == total:
            bond = jnp.where(iota(half.shape, 0) == CHUNK - 1, 0.0, bond)
        down[8 + r0 : 8 + r0 + CHUNK, :] = bond
        if r0 == 0:
            down[7:8, :] = jnp.zeros((1, 128), F32) if ends is None else safe_bond(half[0:1], ends[0])
        before, after = lane_neighbours(half, edge[r0 : r0 + CHUNK, :], field)
        left[r0 : r0 + CHUNK, :] = safe_bond(half, before)
        across[r0 : r0 + CHUNK, :] = safe_bond(half, after)


def chunk_step(now, prev, total, r0, layer, comps, bonds, edge, fields, ends, extra, put):
    down, across, left, thick, coef = bonds
    sl = pl.ds(r0, CHUNK)
    up = down(layer)[pl.ds(7 + r0, CHUNK), :]
    dn = down(layer)[pl.ds(8 + r0, CHUNK), :]
    ac, al, co = across(layer)[sl, :], left(layer)[sl, :], coef(layer)[sl, :]
    for c in range(comps):
        cells, above, below = row_neighbours(now(c, layer), r0, total, None if ends is None else ends(c))
        before, after = lane_neighbours(cells, edge[sl, :], fields(c))
        pull = dn * (below - cells) + up * (above - cells)
        pull = pull + (ac * (after - cells) + al * (before - cells))
        if layer < 5:
            pull = pull + thick(layer)[sl, :] * (now(c, layer + 1)(r0, CHUNK) - cells)
        if layer > 0:
            pull = pull + thick(layer - 1)[sl, :] * (now(c, layer - 1)(r0, CHUNK) - cells)
        if extra is not None:
            pull = pull + extra(c)
        put(c, 2.0 * cells - prev(c, layer)(r0, CHUNK) + co * pull)


def rows_of(ref, *index):
    view = ref.at[index]
    return lambda lo, n: view[pl.ds(lo, n), :]


def ends_of(before, after, index):
    return before[index : index + 1, :], after[index : index + 1, :]


def prep_part(span_ref, chord_ref, stringer_ref, cell_ref, stiff_ref, owner_ref, out_ref, match_ref):
    def row_of(ref):
        return ref[...].reshape(1, -1)

    span, chord, stringer = row_of(span_ref), row_of(chord_ref), row_of(stringer_ref)
    cell, stiff = row_of(cell_ref), row_of(stiff_ref)
    count = span.shape[1]
    chunks = count // 128
    same = iota((48, count), 0) == stringer
    diagonal = iota((48, 48), 0) == iota((48, 48), 1)
    owner = jnp.sum(jnp.where(diagonal, owner_ref[...], 0).astype(F32), axis=1, keepdims=True).astype(jnp.int32)
    slot = jnp.sum(jnp.where(same, owner, 0).astype(F32), axis=0, keepdims=True).astype(jnp.int32)
    foot = (chord - (((2 * cell) * 171) >> 9)) >> 6
    foot_of = jnp.max(jnp.where(same, foot, 0).astype(F32), axis=1, keepdims=True).astype(jnp.int32)
    slots = iota((48, 64), 1)
    slot_hot = (slots == (owner & 1) * 32 + (owner >> 1)).astype(F32).astype(BF16)
    foot_hot = (slots == (foot_of & 1) * 32 + (foot_of >> 1)).astype(F32).astype(BF16)
    match_ref[0:64, 0:64] = lax.dot_general(foot_hot, slot_hot, TN, preferred_element_type=F32)
    match_ref[64:128, 0:64] = lax.dot_general(slot_hot, foot_hot, TN, preferred_element_type=F32)
    one = same.astype(F32)
    lower = (iota((128, 128), 0) < iota((128, 128), 1)).astype(F32).astype(BF16)
    both = jnp.concatenate([lower, jnp.ones((128, 128), BF16)], axis=1)
    offset = jnp.zeros((48, 128), F32)
    ranks = []
    for k in range(chunks):
        part = one[:, k * 128 : (k + 1) * 128]
        ahead = jnp.dot(part.astype(BF16), both, preferred_element_type=F32)
        ranks.append(jnp.sum(part * (ahead[:, :128] + offset), axis=0, keepdims=True))
        offset = offset + ahead[:, 128:]
    rank = jnp.concatenate(ranks, axis=1).astype(jnp.int32)
    place = iota((128, count), 0)
    place = place == jnp.where(
        place < 64, (slot & 1) * 32 + (slot >> 1), 64 + (foot & 1) * 32 + (foot >> 1)
    )
    place = place.astype(F32).astype(BF16)
    order = iota((16, count), 0) == rank
    high = stiff.astype(BF16).astype(F32)
    rest = stiff - high
    middle = rest.astype(BF16).astype(F32)
    fields = [cell.astype(F32), (span & 127).astype(F32), (chord & 127).astype(F32), high, middle, rest - middle]
    rows = jnp.concatenate([pick(order, f) for f in fields], axis=0)
    got = lax.dot_general(place, rows, NT, preferred_element_type=F32)
    for side in range(2):
        index, weight = [], []
        for p in range(2):
            part = got[side * 64 + p * 32 : side * 64 + p * 32 + 32]
            where_, across = part[:, 0:16], part[:, 16:32]
            if side == 1:
                where_, across = part[:, 16:32], part[:, 32:48]
            index.append(where_ * 128.0 + across)
            weight.append(part[:, 48:64] + part[:, 64:80] + part[:, 80:96])
        out_ref[:, side * 64 : side * 64 + 64] = jnp.concatenate(index + weight, axis=1)


def ends_exist():
    span, chord = lax.axis_index("span"), lax.axis_index("chord")
    yes = lambda cond: jnp.where(cond, 1.0, 0.0).astype(F32)
    return (
        yes(span > 0), yes(span < lax.axis_size("span") - 1),
        yes(chord > 0), yes(chord < lax.axis_size("chord") - 1),
    )


def pack_skin(columns, get, layers, r0, first_ref, last_ref):
    for l in layers:
        for c in range(3):
            f = c * 6 + l
            cells = get(c, l)
            columns = with_columns(columns, cells, f)
            if r0 == 0:
                first_ref[f : f + 1, :] = cells[0:1]
            if r0 == 128 - CHUNK:
                last_ref[f : f + 1, :] = cells[CHUNK - 1 : CHUNK]
    return columns


def pack_str(columns, get, layers):
    for p in range(2):
        for t in layers:
            for c in range(3):
                columns = with_columns(columns, get(p, c, t), (p * 3 + c) * 6 + t)
    return columns


def halo_part(stiff_ref, coef_ref, skin_ref, mat_ref, str_ref, smat_ref, last_ref, first_ref, side_ref):
    tabs = tables(stiff_ref, coef_ref)
    at_prev, at_next, at_left, at_right = ends_exist()
    lane = iota((CHUNK, 128), 1)
    side_keep = jnp.where((lane & 1) == 0, at_right, at_left)
    span_keep = jnp.where((lane & 1) == 0, at_next, at_prev)
    for r0 in range(0, 128, CHUNK):
        columns = jnp.zeros((CHUNK, 128), F32)
        for l in range(6):
            half = half_of(mat_ref[l, pl.ds(r0, CHUNK), :], tabs)
            columns = with_columns(columns, half, 18 + l)
            if r0 == 0:
                first_ref[18 + l : 19 + l, :] = half[0:1] * at_prev
            if r0 == 128 - CHUNK:
                last_ref[18 + l : 19 + l, :] = half[CHUNK - 1 : CHUNK] * at_next
        columns = columns * side_keep
        side_ref[pl.ds(r0, CHUNK), :] = pack_skin(
            columns, lambda c, l: skin_ref[c, l, pl.ds(r0, CHUNK), :], range(6), r0, first_ref, last_ref
        )
    for r0 in range(0, 96, CHUNK):
        columns = jnp.zeros((CHUNK, 128), F32)
        for p in range(2):
            for t in range(6):
                half = half_of(smat_ref[p, t, pl.ds(r0, CHUNK), :], tabs)
                columns = with_columns(columns, half, 36 + p * 6 + t)
        columns = columns * span_keep
        columns = pack_str(columns, lambda p, c, t: str_ref[p, c, t, pl.ds(r0, CHUNK), :], range(6))
        last_ref[pl.ds(24 + r0, CHUNK), :] = columns
        first_ref[pl.ds(24 + r0, CHUNK), :] = columns


def opening_body(
    stiff_ref, coef_ref, span_ref, chord_ref, stringer_ref, cell_ref, weight_ref, owner_ref,
    skin_far, mat_far, str_far, smat_far,
    sent_ref, match_ref, last_ref, first_ref, side_ref,
    skin_ref, mat_ref, str_ref, smat_ref, sems,
):
    moves = copies([skin_far, mat_far, str_far, smat_far], [skin_ref, mat_ref, str_ref, smat_ref], sems)
    start(moves)
    prep_part(span_ref, chord_ref, stringer_ref, cell_ref, weight_ref, owner_ref, sent_ref, match_ref)
    finish(moves)
    halo_part(stiff_ref, coef_ref, skin_ref, mat_ref, str_ref, smat_ref, last_ref, first_ref, side_ref)


def exchange(last, first, side):
    def ring(axis):
        count = lax.axis_size(axis)
        return [(i, (i + 1) % count) for i in range(count)]

    back = lambda pairs: [(b, a) for a, b in pairs]
    before = lax.ppermute(last, "span", ring("span"))
    after = lax.ppermute(first, "span", back(ring("span")))
    lefts = lax.ppermute(side, "chord", ring("chord"))
    rights = lax.ppermute(side, "chord", back(ring("chord")))
    return before, after, lefts, rights


def row_lists(index):
    return jnp.concatenate([index[q * 8 : q * 8 + 8, :] for q in range(4)], axis=1)


def one_row(values):
    return jnp.concatenate([values[a : a + 1, :] for a in range(8)], axis=1)


def hots(rows_ref):
    text = one_row(row_lists(rows_ref[:, 0:32])).astype(jnp.int32)
    tk = one_row(row_lists(rows_ref[:, 32:64]))
    sext = one_row(row_lists(rows_ref[:, 64:96])).astype(jnp.int32)
    sk = one_row(row_lists(rows_ref[:, 96:128]))
    slot = ((iota((1, 1024), 1) >> 4) & 1) * 128
    t_row = iota((96, 1024), 0) == (text >> 7)
    t_lane = (iota((256, 1024), 0) == (text & 127) + slot).astype(F32).astype(BF16)
    s_row = iota((128, 1024), 0) == (sext >> 7)
    s_lane = (iota((128, 1024), 0) == (sext & 127)).astype(F32).astype(BF16)
    return (t_row, t_lane, tk), (s_row, s_lane, sk)


def spread(row_mask, lane_hot, values):
    high, low = two_parts(values)
    left = jnp.concatenate([pick(row_mask, high.astype(F32)), pick(row_mask, low.astype(F32))], axis=1)
    right = jnp.concatenate([lane_hot, lane_hot], axis=1)
    return lax.dot_general(left, right, NT, preferred_element_type=F32)


def fetch(row_mask, lane_hot2, cells):
    high, low = two_parts(cells)
    wide = jnp.dot(jnp.concatenate([high, low], axis=1), lane_hot2, preferred_element_type=F32)
    return jnp.sum(jnp.where(row_mask, wide, 0.0), axis=0, keepdims=True)


def as_lanes(row):
    return jnp.concatenate([row[:, a * 128 : (a + 1) * 128] for a in range(8)], axis=0)


def gather_body(
    stiff_ref, coef_ref, rows_ref, skin_ref, skin_prev_ref, mat_ref, str_ref, str_prev_ref, smat_ref,
    before_ref, after_ref, lefts_ref, rights_ref, later_ref,
    out_ref, ks_ref, ps_ref, cs_ref, kt_ref, pt_ref, ct_ref,
    half_ref, down_ref, across_ref, left_ref, thick_ref, edge_ref, tedge_ref, co_ref,
):
    tabs = tables(stiff_ref, coef_ref)
    (t_row, t_lane, tk), (s_row, s_lane, sk) = hots(rows_ref)
    ks_ref[...] = spread(s_row, s_lane, sk)
    kt_ref[...] = spread(t_row, t_lane, tk)
    edge_ref[...] = joined(lefts_ref[...], rights_ref[...])
    tedge_ref[...] = joined(before_ref[24:120, :], after_ref[24:120, :])
    bonds = (lambda l: down_ref, lambda l: across_ref, lambda l: left_ref, lambda l: thick_ref, lambda l: co_ref)

    def prepare(total, own, other, ends, edge, field):
        for r0 in range(0, total, CHUNK):
            sl = pl.ds(r0, CHUNK)
            half, coef = half_coef(own[sl, :], tabs)
            half_ref[sl, :] = half
            co_ref[sl, :] = coef
            thick_ref[sl, :] = 1.0 / (half + half_of(other[sl, :], tabs))
        layer_bonds(lambda lo, n: half_ref[pl.ds(lo, n), :], total, ends, edge, field, down_ref, across_ref, left_ref)

    prepare(128, mat_ref.at[1], mat_ref.at[0], ends_of(before_ref, after_ref, 23), edge_ref, 23)
    cs_ref[...] = co_ref[...]
    for r0 in range(0, 128, CHUNK):
        sl = pl.ds(r0, CHUNK)

        def put(c, value):
            ps_ref[c, sl, :] = value - cs_ref[sl, :] * ks_ref[sl, :] * skin_ref[c, 1, sl, :]

        chunk_step(
            lambda c, l: rows_of(skin_ref, c, l - 4), lambda c, l: rows_of(skin_prev_ref, c, 0), 128, r0, 5, 3, bonds,
            edge_ref, lambda c: c * 6 + 5, lambda c: ends_of(before_ref, after_ref, c * 6 + 5), None, put,
        )
    for p in range(2):
        prepare(96, smat_ref.at[p, 0], smat_ref.at[p, 1], None, tedge_ref, 36 + p * 6)
        lanes = pl.ds(p * 128, 128)
        ct_ref[:, p * 128 : p * 128 + 128] = co_ref[0:96, :]
        for r0 in range(0, 96, CHUNK):
            sl = pl.ds(r0, CHUNK)

            def put(c, value):
                pt_ref[c, sl, lanes] = value - ct_ref[sl, lanes] * kt_ref[sl, lanes] * str_ref[p, c, 0, sl, :]

            chunk_step(
                lambda c, l: rows_of(str_ref, p, c, l), lambda c, l: rows_of(str_prev_ref, p, c, l), 96, r0, 0, 3, bonds,
                tedge_ref, lambda c: (p * 3 + c) * 6, None, None, put,
            )
    t_fields = [jnp.concatenate([str_ref[0, c, 0], str_ref[1, c, 0]], axis=1) for c in range(3)]
    t_fields += [pt_ref[c] for c in range(3)] + [ct_ref[...] * kt_ref[...]]
    s_fields = [skin_ref[c, 1] for c in range(3)] + [ps_ref[c] for c in range(3)] + [cs_ref[...]]
    t_two = jnp.concatenate([t_lane, t_lane], axis=0)
    s_two = jnp.concatenate([s_lane, s_lane], axis=0)
    got = [as_lanes(fetch(t_row, t_two, f)) for f in t_fields]
    got += [as_lanes(fetch(s_row, s_two, f)) for f in s_fields]
    pad = jnp.zeros((8, 128), F32)
    got += [pad, pad]
    for j in range(4):
        part = [
            jnp.concatenate([g[:, q * 32 : q * 32 + 32] for g in got[4 * j : 4 * j + 4]], axis=1) for q in range(4)
        ]
        out_ref[pl.ds(j, 32, stride=4), :] = jnp.concatenate(part, axis=0)


def bounce_body(match_ref, got_ref, later_ref, out_ref):
    got = jnp.concatenate([got_ref[pl.ds(j, 32, stride=4), :] for j in range(4)], axis=1)
    lane = iota(got.shape, 1)
    zero = (lane & 16) == 0

    def turned(base):
        def part(to, frm):
            m = match_ref[base + to * 32 : base + to * 32 + 32, frm * 32 : frm * 32 + 32]
            return jnp.dot(m, got, preferred_element_type=F32, precision=lax.Precision.HIGHEST)

        a = part(0, 0) + pltpu.roll(part(0, 1), 512 - 16, 1)
        b = part(1, 1) + pltpu.roll(part(1, 0), 16, 1)
        return jnp.where(zero, a, b)

    new = jnp.where(lane < FIELDS * 32, turned(0), turned(64))
    for j in range(4):
        out_ref[pl.ds(j, 32, stride=4), :] = new[:, j * 128 : j * 128 + 128]


def spread_all(row_mask, lane_hot_t, values):
    rows = []
    for value in values:
        high, low = two_parts(value)
        rows.append(jnp.concatenate([pick(row_mask, high.astype(F32)), pick(row_mask, low.astype(F32))], axis=1))
    count = row_mask.shape[0]
    got = jnp.dot(
        jnp.concatenate(rows, axis=0), jnp.concatenate([lane_hot_t, lane_hot_t], axis=0), preferred_element_type=F32
    )
    return [got[f * count : f * count + count] for f in range(len(values))]


def load_body(
    rows_ref, posted_ref, ks_ref, ps_ref, cs_ref, kt_ref, pt_ref, ct_ref, skin_ref, str_ref,
    last_in, first_in, side_in, columns_in,
    skin1_ref, sload_ref, str1_ref, tload_ref, last_ref, first_ref, side_ref,
):
    (t_row, t_lane, tk), (s_row, s_lane, sk) = hots(rows_ref)
    posted = [posted_ref[pl.ds(j, 32, stride=4), :] for j in range(4)]

    def sums(side, row_mask, lane_hot, weight):
        values = []
        for f in range(FIELDS):
            g = side * FIELDS + f
            at = g % 4 * 32
            values.append(weight * one_row(row_lists(posted[g // 4][:, at : at + 32])))
        return spread_all(row_mask, lane_hot.astype(F32).T.astype(BF16), values)

    last_ref[0:24, :] = last_in[...]
    first_ref[0:24, :] = first_in[...]
    side = side_in[...]
    ks, cs = ks_ref[...], cs_ref[...]
    got = sums(0, s_row, s_lane, sk)
    for c in range(3):
        now = skin_ref[c, 0]
        new = ps_ref[c] + cs * got[c]
        skin1_ref[c] = new
        sload_ref[c] = got[3 + c] + got[6] * now - ks * new
        f = c * 6 + 5
        last_ref[f : f + 1, :] = new[127:128, :]
        first_ref[f : f + 1, :] = new[0:1, :]
        side = with_columns(side, new, f)
    side_ref[...] = side
    kt, ct = kt_ref[...], ct_ref[...]
    got = sums(1, t_row, t_lane, tk)
    third = iota((96, 256), 0) % 3
    columns = columns_in[...]
    for c in range(3):
        now = jnp.concatenate([str_ref[0, c, 0], str_ref[1, c, 0]], axis=1)
        own = kt * now
        pair = jnp.where(third == 0, pltpu.roll(own, 95, 0), jnp.where(third == 1, pltpu.roll(own, 1, 0), 0.0))
        new = pt_ref[c] + ct * got[c]
        load = got[3 + c] + got[6] * (own + pair) - kt * new
        for p in range(2):
            str1_ref[p, c] = new[:, p * 128 : p * 128 + 128]
            tload_ref[p, c] = load[:, p * 128 : p * 128 + 128]
            columns = with_columns(columns, new[:, p * 128 : p * 128 + 128], (p * 3 + c) * 6)
    last_ref[24:120, :] = columns
    first_ref[24:120, :] = columns


def bonds_body(
    stiff_ref, coef_ref, mat_ref, smat_ref, before_ref, after_ref, lefts_ref, rights_ref,
    sd_ref, sa_ref, sl_ref, st_ref, sc_ref, td_ref, ta_ref, tl_ref, tt_ref, tc_ref,
    sh_ref, th_ref, edge_ref, tedge_ref,
):
    tabs = tables(stiff_ref, coef_ref)
    edge_ref[...] = joined(lefts_ref[...], rights_ref[...])
    tedge_ref[...] = joined(before_ref[24:120, :], after_ref[24:120, :])
    for r0 in range(0, 128, CHUNK):
        sl = pl.ds(r0, CHUNK)
        for l in range(6):
            half, coef = half_coef(mat_ref[l, sl, :], tabs)
            if l > 0:
                st_ref[l - 1, sl, :] = 1.0 / (half + sh_ref[l - 1, sl, :])
            sh_ref[l, sl, :] = half
            sc_ref[l, sl, :] = coef
    for l in range(6):
        layer_bonds(
            rows_of(sh_ref, l), 128, ends_of(before_ref, after_ref, 18 + l), edge_ref, 18 + l,
            sd_ref.at[l], sa_ref.at[l], sl_ref.at[l],
        )
    for p in range(2):
        for r0 in range(0, 96, CHUNK):
            sl = pl.ds(r0, CHUNK)
            for t in range(6):
                half, coef = half_coef(smat_ref[p, t, sl, :], tabs)
                if t > 0:
                    tt_ref[p, t - 1, sl, :] = 1.0 / (half + th_ref[t - 1, sl, :])
                th_ref[t, sl, :] = half
                tc_ref[p, t, sl, :] = coef
        for t in range(6):
            layer_bonds(
                rows_of(th_ref, t), 96, None, tedge_ref, 36 + p * 6 + t, td_ref.at[p, t], ta_ref.at[p, t], tl_ref.at[p, t]
            )


def skin_chunks(now, prev, bonds, edge_ref, before_ref, after_ref, layers, extra, put):
    for r0 in range(0, 128, CHUNK):
        for l in layers:
            chunk_step(
                now, prev, 128, r0, l, 3, bonds, edge_ref, lambda c: c * 6 + l,
                lambda c: ends_of(before_ref, after_ref, c * 6 + l),
                (lambda c: extra(c, r0)) if l == 5 and extra is not None else None, lambda c, v: put(c, l, r0, v),
            )


def str_chunks(now, prev, bonds, edge_ref, layers, extra, put, done=None):
    for p in range(2):
        for r0 in range(0, 96, CHUNK):
            for t in layers:
                chunk_step(
                    lambda c, m: now(p, c, m), lambda c, m: prev(p, c, m), 96, r0, t, 3, bonds(p), edge_ref,
                    lambda c: (p * 3 + c) * 6 + t, None,
                    (lambda c: extra(p, c, r0)) if t == 0 and extra is not None else None,
                    lambda c, v: put(p, c, t, r0, v),
                )
        if done is not None:
            done(p)


def at_layers(*refs):
    return tuple((lambda l, ref=ref: ref.at[l]) for ref in refs)


def first_skin_body(*refs):
    far, (skin1_far, last_ref, first_ref, side_ref), near_refs = refs[:11], refs[12:16], refs[16:27]
    skin1_ref, edge_ref, sems = refs[27:]
    skin_ref, skin_prev_ref, before_ref, after_ref, lefts_ref, rights_ref, sd_ref, sa_ref, sl_ref, st_ref, sc_ref = near_refs
    moves = copies(far, near_refs, sems)
    start(moves)
    finish(moves)
    edge_ref[...] = joined(lefts_ref[...], rights_ref[...])
    last_ref[...] = jnp.zeros((24, 128), F32)
    first_ref[...] = jnp.zeros((24, 128), F32)

    def put_skin(c, l, r0, value):
        skin1_ref[c, l, pl.ds(r0, CHUNK), :] = value

    skin_chunks(
        lambda c, l: rows_of(skin_ref, c, l), lambda c, l: rows_of(skin_prev_ref, c, l),
        at_layers(sd_ref, sa_ref, sl_ref, st_ref, sc_ref), edge_ref, before_ref, after_ref, range(5), None, put_skin,
    )
    out = copies([skin1_ref], [skin1_far], sems, 11)
    start(out)
    for r0 in range(0, 128, CHUNK):
        side_ref[pl.ds(r0, CHUNK), :] = pack_skin(
            jnp.zeros((CHUNK, 128), F32), lambda c, l: skin1_ref[c, l, pl.ds(r0, CHUNK), :], range(5), r0, first_ref, last_ref
        )
    finish(out)


def first_str_body(*refs):
    far, (str1_far, columns_ref), near_refs = refs[:9], refs[10:12], refs[12:21]
    str1_ref, tedge_ref, sems = refs[21:]
    str_ref, str_prev_ref, before_ref, after_ref, td_ref, ta_ref, tl_ref, tt_ref, tc_ref = near_refs
    moves = [
        copies([f.at[p] for f in far[:2] + far[4:]], [n.at[p] for n in near_refs[:2] + near_refs[4:]], sems, 7 * p)
        for p in range(2)
    ]
    ends = copies(far[2:4], near_refs[2:4], sems, 14)
    start(ends + moves[0] + moves[1])
    finish(ends + moves[0])
    tedge_ref[...] = joined(before_ref[24:120, :], after_ref[24:120, :])
    out = copies([str1_ref.at[0], str1_ref.at[1]], [str1_far.at[0], str1_far.at[1]], sems, 16)

    def put_str(p, c, t, r0, value):
        str1_ref[p, c, t - 1, pl.ds(r0, CHUNK), :] = value

    def done(p):
        out[p].start()
        if p == 0:
            finish(moves[1])

    str_chunks(
        lambda p, c, t: rows_of(str_ref, p, c, t), lambda p, c, t: rows_of(str_prev_ref, p, c, t),
        lambda p: at_layers(*(r.at[p] for r in (td_ref, ta_ref, tl_ref, tt_ref, tc_ref))), tedge_ref, range(1, 6), None,
        put_str, done,
    )
    for r0 in range(0, 96, CHUNK):
        columns_ref[pl.ds(r0, CHUNK), :] = pack_str(
            jnp.zeros((CHUNK, 128), F32), lambda p, c, t: str1_ref[p, c, t - 1, pl.ds(r0, CHUNK), :], range(1, 6)
        )
    finish(out)


def second_body(*refs):
    far, (skin2_far, str2_far), near_refs = refs[:22], refs[22:24], refs[24:46]
    skin2_ref, str2_ref, edge_ref, tedge_ref, sems = refs[46:]
    moves = copies(far, near_refs, sems)
    (
        skin_ref, skin_prev_ref, str_ref, str_prev_ref, before_ref, after_ref, lefts_ref, rights_ref,
        sd_ref, sa_ref, sl_ref, st_ref, sc_ref, td_ref, ta_ref, tl_ref, tt_ref, tc_ref,
        skin_face_ref, str_face_ref, sload_ref, tload_ref,
    ) = near_refs
    skin_moves = [moves[i] for i in (4, 5, 6, 7, 8, 9, 10, 11, 12, 0, 1, 18, 20)]
    str_moves = [moves[i] for i in (13, 14, 15, 16, 17, 2, 3, 19, 21)]
    start(skin_moves + str_moves)
    finish(skin_moves)
    edge_ref[...] = joined(lefts_ref[...], rights_ref[...])
    tedge_ref[...] = joined(before_ref[24:120, :], after_ref[24:120, :])

    def put_skin(c, l, r0, value):
        skin2_ref[c, l, pl.ds(r0, CHUNK), :] = value

    def put_str(p, c, t, r0, value):
        str2_ref[p, c, t, pl.ds(r0, CHUNK), :] = value

    skin_chunks(
        lambda c, l: rows_of(skin_face_ref, c) if l == 5 else rows_of(skin_ref, c, l),
        lambda c, l: rows_of(skin_prev_ref, c, l),
        at_layers(sd_ref, sa_ref, sl_ref, st_ref, sc_ref), edge_ref, before_ref, after_ref, range(6),
        lambda c, r0: sload_ref[c, pl.ds(r0, CHUNK), :], put_skin,
    )
    out_moves = copies([skin2_ref, str2_ref.at[0], str2_ref.at[1]], [skin2_far, str2_far.at[0], str2_far.at[1]], sems, 22)
    out_moves[0].start()
    finish(str_moves)
    str_chunks(
        lambda p, c, t: rows_of(str_face_ref, p, c) if t == 0 else rows_of(str_ref, p, c, t - 1),
        lambda p, c, t: rows_of(str_prev_ref, p, c, t),
        lambda p: at_layers(*(r.at[p] for r in (td_ref, ta_ref, tl_ref, tt_ref, tc_ref))), tedge_ref, range(6),
        lambda p, c, r0: tload_ref[p, c, pl.ds(r0, CHUNK), :], put_str, lambda p: out_moves[1 + p].start(),
    )
    finish(out_moves)


def swap(values):
    peers = lax.axis_size("chord")
    moved = lax.all_to_all(values.reshape(peers, -1, 128), "chord", split_axis=0, concat_axis=0, tiled=True)
    return moved.reshape(values.shape)


def shards(
    skin_now, skin_prev, skin_mat, stringer_now, stringer_prev, stringer_mat, owner_slot,
    rivet_span, rivet_chord, rivet_stringer, rivet_cell, rivet_stiff, mat_stiff, mat_coef,
):
    mats = [mat_stiff, mat_coef]
    own = [skin_now, skin_mat, stringer_now, stringer_mat]
    column = [(120, 128), (120, 128), (128, 128)]
    sent, match, *packs = call(
        opening_body, [(32, 128), (128, 128), *column],
        [*mats, rivet_span, rivet_chord, rivet_stringer, rivet_cell, rivet_stiff, owner_slot.reshape(1, -1), *own],
        "opening", smem=(0, 1), far=range(8, 12), flops=4000000, nbytes=4000000, scratch=near(own), sems=4,
    )
    rows = swap(sent)
    halos = exchange(*packs)
    edges = [(128, 128), (96, 128)]
    bonds = call(
        bonds_body, [(6, 136, 128), *[(6, 128, 128)] * 4, (2, 6, 104, 128), *[(2, 6, 96, 128)] * 4],
        [*mats, skin_mat, stringer_mat, *halos], "bonds", smem=(0, 1), flops=10000000, nbytes=8000000,
        scratch=floats((6, 128, 128), (6, 96, 128), *edges),
    )
    found, *kept = call(
        gather_body, [(128, 128), (128, 128), (3, 128, 128), (128, 128), (96, 256), (3, 96, 256), (96, 256)],
        [*mats, rows, skin_now, skin_prev, skin_mat, stringer_now, stringer_prev, stringer_mat, *halos, bonds[0]], "gather",
        smem=(0, 1), far=(13,), flops=1000000000, nbytes=2000000,
        views={
            3: ((3, 2, 128, 128), (0, 2, 0, 0)),
            4: ((3, 1, 128, 128), (0, 5, 0, 0)),
            5: ((2, 128, 128), (2, 0, 0)),
            6: ((2, 3, 2, 96, 128), (0, 0, 0, 0, 0)),
            7: ((2, 3, 1, 96, 128), (0, 0, 0, 0, 0)),
            8: ((2, 2, 96, 128), (0, 0, 0, 0)),
        },
        scratch=floats((128, 128), (136, 128), (128, 128), (128, 128), (128, 128), *edges, (128, 128)),
    )
    given = swap(found)
    parts = [skin_now, skin_prev, *halos, *bonds[:5]]
    skin1, last, first, side = call(
        first_skin_body, [(3, 5, 128, 128), (24, 128), (24, 128), (128, 128)], [*parts, found], "first_skin",
        far=range(12), far_outs=(0,), flops=10000000, nbytes=5000000,
        scratch=near(parts) + floats((3, 5, 128, 128), (128, 128)), sems=12,
    )
    (turned,) = call(bounce_body, [(128, 128)], [match, given, last], "bounce", fast=(1,), far=(2,), limit=8)
    posted = swap(turned)
    parts = [stringer_now, stringer_prev, *halos[:2], *bonds[5:]]
    str1, columns = call(
        first_str_body, [(2, 3, 5, 96, 128), (96, 128)], [*parts, turned], "first_str",
        far=range(10), far_outs=(0,), flops=10000000, nbytes=5000000,
        scratch=near(parts) + floats((2, 3, 5, 96, 128), (96, 128)), sems=18,
    )
    skin_face, sload, str_face, tload, *packs2 = call(
        load_body, [(3, 128, 128), (3, 128, 128), (2, 3, 96, 128), (2, 3, 96, 128), *column],
        [rows, posted, *kept, skin_now, stringer_now, last, first, side, columns], "load", flops=1000000000, nbytes=2000000,
        views={8: ((3, 1, 128, 128), (0, 5, 0, 0)), 9: ((2, 3, 1, 96, 128), (0, 0, 0, 0, 0))},
    )
    halos1 = exchange(*packs2)
    parts = [skin1, skin_now, str1, stringer_now, *halos1, *bonds, skin_face, str_face, sload, tload]
    results = [(3, 6, 128, 128), (2, 3, 6, 96, 128)]
    return call(
        second_body, results, parts, "second", far=range(22), far_outs=(0, 1), flops=20000000, nbytes=10000000,
        scratch=near(parts) + floats(*results, *edges), sems=25, limit=56,
    )


def solution(mesh):
    placed = (
        P(None, None, "span", "chord"),
        P(None, None, "span", "chord"),
        P(None, "span", "chord"),
        P("chord", None, None, None, "span"),
        P("chord", None, None, None, "span"),
        P("chord", None, None, "span"),
        P(),
        P(("span", "chord")),
        P(("span", "chord")),
        P(("span", "chord")),
        P(("span", "chord")),
        P(("span", "chord")),
        P(),
        P(),
    )
    body = jax.shard_map(
        shards,
        mesh=mesh,
        in_specs=placed,
        out_specs=(P(None, None, "span", "chord"), P("chord", None, None, None, "span")),
        check_vma=False,
    )
    return lambda *args: tuple(body(*args))
```

```python
import jax
import jax.numpy as jnp
from jax import lax
from jax.experimental import pallas as pl
from jax.experimental.pallas import tpu as pltpu
from jax.sharding import PartitionSpec as P

F32 = jnp.float32
BF16 = jnp.bfloat16
NT = (((1,), (1,)), ((), ()))
TN = (((0,), (0,)), ((), ()))
FIELDS = 7


def iota(shape, dim):
    return lax.broadcasted_iota(jnp.int32, shape, dim)


def two_parts(values):
    high = values.astype(BF16)
    return high, (values - high.astype(F32)).astype(BF16)


def pick(mask, values):
    return jnp.where(mask, values, 0.0).astype(BF16)


def whole(shape):
    return pl.BlockSpec(tuple(shape), lambda i: (0,) * len(shape), pipeline_mode=pl.Buffered(1))


def call(body, outs, ins, name, smem=(), far=(), fast=(), views=None, far_outs=(), flops=0, nbytes=0, scratch=(), sems=0, limit=56):
    views = views or {}

    def spec(i, a):
        if i in smem:
            return pl.BlockSpec(memory_space=pltpu.SMEM)
        if i in far:
            return pl.BlockSpec(memory_space=pl.ANY)
        if i in fast:
            return pl.BlockSpec(memory_space=pltpu.VMEM)
        if i in views:
            shape, at = views[i]
            return pl.BlockSpec(shape, lambda g: at)
        return whole(a.shape)

    return pl.pallas_call(
        body,
        grid=(1,),
        out_shape=[jax.ShapeDtypeStruct(s, F32) for s in outs],
        in_specs=[spec(i, a) for i, a in enumerate(ins)],
        out_specs=[pl.BlockSpec(memory_space=pl.ANY) if i in far_outs else whole(s) for i, s in enumerate(outs)],
        scratch_shapes=[pltpu.VMEM(s, t) for s, t in scratch] + ([pltpu.SemaphoreType.DMA((sems,))] if sems else []),
        compiler_params=pltpu.CompilerParams(vmem_limit_bytes=limit * 1024 * 1024),
        cost_estimate=pl.CostEstimate(flops=flops, bytes_accessed=nbytes, transcendentals=0),
        name=name,
    )(*ins)


def gate(moves):
    waited = set()

    def need(*keys):
        for key in keys:
            if key in moves and key not in waited:
                waited.add(key)
                moves[key].wait()

    return need


def near(arrays):
    return [(a.shape, a.dtype) for a in arrays]


def floats(*shapes):
    return [(s, F32) for s in shapes]


def copies(sources, targets, sems, at=0):
    return [pltpu.make_async_copy(s, t, sems.at[at + i]) for i, (s, t) in enumerate(zip(sources, targets))]


def start(moves):
    for move in moves:
        move.start()


def finish(moves):
    for move in moves:
        move.wait()


def tables(stiff_ref, coef_ref):
    half = [0.5 / jnp.full((1, 128), stiff_ref[m], F32) for m in range(8)]
    return half, [coef_ref[m] for m in range(8)]


def half_of(mat, tabs):
    out = jnp.broadcast_to(tabs[0][0], mat.shape)
    for m in range(1, 8):
        out = jnp.where(mat == m, tabs[0][m], out)
    return out


def half_coef(mat, tabs):
    half = jnp.broadcast_to(tabs[0][0], mat.shape)
    coef = jnp.full(mat.shape, tabs[1][0], F32)
    for m in range(1, 8):
        same = mat == m
        half = jnp.where(same, tabs[0][m], half)
        coef = jnp.where(same, tabs[1][m], coef)
    return half, coef


CHUNK = 32


def joined(before, after):
    lane = iota(before.shape, 1)
    return jnp.where((lane & 1) == 1, pltpu.roll(before, 1, 1), pltpu.roll(after, 127, 1))


def with_columns(columns, cells, field):
    lane = iota(cells.shape, 1)
    return jnp.where((lane >> 1) == field, pltpu.roll(cells, 2 * field + 1, 1), columns)


def row_neighbours(get, r0, total, ends):
    cells = get(r0, CHUNK)
    row = iota(cells.shape, 0)
    if r0 > 0:
        above = get(r0 - 1, CHUNK)
    else:
        above = pltpu.roll(cells, 1, 0)
        if ends is not None:
            above = jnp.where(row == 0, ends[0], above)
    if r0 + CHUNK < total:
        below = get(r0 + 1, CHUNK)
    else:
        below = pltpu.roll(cells, CHUNK - 1, 0)
        if ends is not None:
            below = jnp.where(row == CHUNK - 1, ends[1], below)
    return cells, above, below


def lane_neighbours(cells, edge, field):
    lane = iota(cells.shape, 1)
    turned = pltpu.roll(edge, (127 - 2 * field) % 128, 1)
    before = jnp.where(lane == 0, turned, pltpu.roll(cells, 1, 1))
    after = jnp.where(lane == 127, turned, pltpu.roll(cells, 127, 1))
    return before, after


def safe_bond(half, beside):
    return jnp.where(beside > 0.0, 1.0 / (half + beside), 0.0)


def layer_bonds(get, total, ends, edge, field, down, across, left):
    for r0 in range(0, total, CHUNK):
        half, _, below = row_neighbours(get, r0, total, ends)
        bond = safe_bond(half, below)
        if ends is None and r0 + CHUNK == total:
            bond = jnp.where(iota(half.shape, 0) == CHUNK - 1, 0.0, bond)
        down[8 + r0 : 8 + r0 + CHUNK, :] = bond
        if r0 == 0:
            down[7:8, :] = jnp.zeros((1, 128), F32) if ends is None else safe_bond(half[0:1], ends[0])
        before, after = lane_neighbours(half, edge[r0 : r0 + CHUNK, :], field)
        left[r0 : r0 + CHUNK, :] = safe_bond(half, before)
        across[r0 : r0 + CHUNK, :] = safe_bond(half, after)


def chunk_step(now, prev, total, r0, layer, comps, bonds, edge, fields, ends, extra, put):
    down, across, left, thick, coef = bonds
    sl = pl.ds(r0, CHUNK)
    up = down(layer)[pl.ds(7 + r0, CHUNK), :]
    dn = down(layer)[pl.ds(8 + r0, CHUNK), :]
    ac, al, co = across(layer)[sl, :], left(layer)[sl, :], coef(layer)[sl, :]
    for c in range(comps):
        cells, above, below = row_neighbours(now(c, layer), r0, total, None if ends is None else ends(c))
        before, after = lane_neighbours(cells, edge[sl, :], fields(c))
        pull = dn * (below - cells) + up * (above - cells)
        pull = pull + (ac * (after - cells) + al * (before - cells))
        if layer < 5:
            pull = pull + thick(layer)[sl, :] * (now(c, layer + 1)(r0, CHUNK) - cells)
        if layer > 0:
            pull = pull + thick(layer - 1)[sl, :] * (now(c, layer - 1)(r0, CHUNK) - cells)
        if extra is not None:
            pull = pull + extra(c)
        put(c, 2.0 * cells - prev(c, layer)(r0, CHUNK) + co * pull)


def rows_of(ref, *index):
    view = ref.at[index]
    return lambda lo, n: view[pl.ds(lo, n), :]


def ends_of(before, after, index):
    return before[index : index + 1, :], after[index : index + 1, :]


def prep_part(span_ref, chord_ref, stringer_ref, cell_ref, stiff_ref, owner_ref, out_ref, match_ref):
    def row_of(ref):
        return ref[...].reshape(1, -1)

    span, chord, stringer = row_of(span_ref), row_of(chord_ref), row_of(stringer_ref)
    cell, stiff = row_of(cell_ref), row_of(stiff_ref)
    count = span.shape[1]
    chunks = count // 128
    same = iota((48, count), 0) == stringer
    diagonal = iota((48, 48), 0) == iota((48, 48), 1)
    owner = jnp.sum(jnp.where(diagonal, owner_ref[...], 0).astype(F32), axis=1, keepdims=True).astype(jnp.int32)
    slot = jnp.sum(jnp.where(same, owner, 0).astype(F32), axis=0, keepdims=True).astype(jnp.int32)
    foot = (chord - (((2 * cell) * 171) >> 9)) >> 6
    foot_of = jnp.max(jnp.where(same, foot, 0).astype(F32), axis=1, keepdims=True).astype(jnp.int32)
    slots = iota((48, 64), 1)
    slot_hot = (slots == (owner & 1) * 32 + (owner >> 1)).astype(F32).astype(BF16)
    foot_hot = (slots == (foot_of & 1) * 32 + (foot_of >> 1)).astype(F32).astype(BF16)
    match_ref[0:64, 0:64] = lax.dot_general(foot_hot, slot_hot, TN, preferred_element_type=F32)
    match_ref[64:128, 0:64] = lax.dot_general(slot_hot, foot_hot, TN, preferred_element_type=F32)
    one = same.astype(F32)
    lower = (iota((128, 128), 0) < iota((128, 128), 1)).astype(F32).astype(BF16)
    both = jnp.concatenate([lower, jnp.ones((128, 128), BF16)], axis=1)
    offset = jnp.zeros((48, 128), F32)
    ranks = []
    for k in range(chunks):
        part = one[:, k * 128 : (k + 1) * 128]
        ahead = jnp.dot(part.astype(BF16), both, preferred_element_type=F32)
        ranks.append(jnp.sum(part * (ahead[:, :128] + offset), axis=0, keepdims=True))
        offset = offset + ahead[:, 128:]
    rank = jnp.concatenate(ranks, axis=1).astype(jnp.int32)
    place = iota((128, count), 0)
    place = place == jnp.where(
        place < 64, (slot & 1) * 32 + (slot >> 1), 64 + (foot & 1) * 32 + (foot >> 1)
    )
    place = place.astype(F32).astype(BF16)
    order = iota((16, count), 0) == rank
    high = stiff.astype(BF16).astype(F32)
    rest = stiff - high
    middle = rest.astype(BF16).astype(F32)
    fields = [cell.astype(F32), (span & 127).astype(F32), (chord & 127).astype(F32), high, middle, rest - middle]
    rows = jnp.concatenate([pick(order, f) for f in fields], axis=0)
    got = lax.dot_general(place, rows, NT, preferred_element_type=F32)
    for side in range(2):
        index, weight = [], []
        for p in range(2):
            part = got[side * 64 + p * 32 : side * 64 + p * 32 + 32]
            where_, across = part[:, 0:16], part[:, 16:32]
            if side == 1:
                where_, across = part[:, 16:32], part[:, 32:48]
            index.append(where_ * 128.0 + across)
            weight.append(part[:, 48:64] + part[:, 64:80] + part[:, 80:96])
        out_ref[:, side * 64 : side * 64 + 64] = jnp.concatenate(index + weight, axis=1)


def ends_exist():
    span, chord = lax.axis_index("span"), lax.axis_index("chord")
    yes = lambda cond: jnp.where(cond, 1.0, 0.0).astype(F32)
    return (
        yes(span > 0), yes(span < lax.axis_size("span") - 1),
        yes(chord > 0), yes(chord < lax.axis_size("chord") - 1),
    )


def pack_skin(columns, get, layers, r0, first_ref, last_ref):
    for l in layers:
        for c in range(3):
            f = c * 6 + l
            cells = get(c, l)
            columns = with_columns(columns, cells, f)
            if r0 == 0:
                first_ref[f : f + 1, :] = cells[0:1]
            if r0 == 128 - CHUNK:
                last_ref[f : f + 1, :] = cells[CHUNK - 1 : CHUNK]
    return columns


def pack_str(columns, get, layers):
    for p in range(2):
        for t in layers:
            for c in range(3):
                columns = with_columns(columns, get(p, c, t), (p * 3 + c) * 6 + t)
    return columns


def halo_part(stiff_ref, coef_ref, skin_ref, mat_ref, str_ref, smat_ref, last_ref, first_ref, side_ref):
    tabs = tables(stiff_ref, coef_ref)
    at_prev, at_next, at_left, at_right = ends_exist()
    lane = iota((CHUNK, 128), 1)
    side_keep = jnp.where((lane & 1) == 0, at_right, at_left)
    span_keep = jnp.where((lane & 1) == 0, at_next, at_prev)
    for r0 in range(0, 128, CHUNK):
        columns = jnp.zeros((CHUNK, 128), F32)
        for l in range(6):
            half = half_of(mat_ref[l, pl.ds(r0, CHUNK), :], tabs)
            columns = with_columns(columns, half, 18 + l)
            if r0 == 0:
                first_ref[18 + l : 19 + l, :] = half[0:1] * at_prev
            if r0 == 128 - CHUNK:
                last_ref[18 + l : 19 + l, :] = half[CHUNK - 1 : CHUNK] * at_next
        columns = columns * side_keep
        side_ref[pl.ds(r0, CHUNK), :] = pack_skin(
            columns, lambda c, l: skin_ref[c, l, pl.ds(r0, CHUNK), :], range(6), r0, first_ref, last_ref
        )
    for r0 in range(0, 96, CHUNK):
        columns = jnp.zeros((CHUNK, 128), F32)
        for p in range(2):
            for t in range(6):
                half = half_of(smat_ref[p, t, pl.ds(r0, CHUNK), :], tabs)
                columns = with_columns(columns, half, 36 + p * 6 + t)
        columns = columns * span_keep
        columns = pack_str(columns, lambda p, c, t: str_ref[p, c, t, pl.ds(r0, CHUNK), :], range(6))
        last_ref[pl.ds(24 + r0, CHUNK), :] = columns
        first_ref[pl.ds(24 + r0, CHUNK), :] = columns


def opening_body(
    stiff_ref, coef_ref, span_ref, chord_ref, stringer_ref, cell_ref, weight_ref, owner_ref,
    skin_far, mat_far, str_far, smat_far,
    sent_ref, match_ref, last_ref, first_ref, side_ref,
    skin_ref, mat_ref, str_ref, smat_ref, sems,
):
    moves = copies([skin_far, mat_far, str_far, smat_far], [skin_ref, mat_ref, str_ref, smat_ref], sems)
    start(moves)
    prep_part(span_ref, chord_ref, stringer_ref, cell_ref, weight_ref, owner_ref, sent_ref, match_ref)
    finish(moves)
    halo_part(stiff_ref, coef_ref, skin_ref, mat_ref, str_ref, smat_ref, last_ref, first_ref, side_ref)


def exchange(last, first, side):
    def ring(axis):
        count = lax.axis_size(axis)
        return [(i, (i + 1) % count) for i in range(count)]

    back = lambda pairs: [(b, a) for a, b in pairs]
    before = lax.ppermute(last, "span", ring("span"))
    after = lax.ppermute(first, "span", back(ring("span")))
    lefts = lax.ppermute(side, "chord", ring("chord"))
    rights = lax.ppermute(side, "chord", back(ring("chord")))
    return before, after, lefts, rights


def row_lists(index):
    return jnp.concatenate([index[q * 8 : q * 8 + 8, :] for q in range(4)], axis=1)


def one_row(values):
    return jnp.concatenate([values[a : a + 1, :] for a in range(8)], axis=1)


def hots(rows_ref):
    text = one_row(row_lists(rows_ref[:, 0:32])).astype(jnp.int32)
    tk = one_row(row_lists(rows_ref[:, 32:64]))
    sext = one_row(row_lists(rows_ref[:, 64:96])).astype(jnp.int32)
    sk = one_row(row_lists(rows_ref[:, 96:128]))
    slot = ((iota((1, 1024), 1) >> 4) & 1) * 128
    t_row = iota((96, 1024), 0) == (text >> 7)
    t_lane = (iota((256, 1024), 0) == (text & 127) + slot).astype(F32).astype(BF16)
    s_row = iota((128, 1024), 0) == (sext >> 7)
    s_lane = (iota((128, 1024), 0) == (sext & 127)).astype(F32).astype(BF16)
    return (t_row, t_lane, tk), (s_row, s_lane, sk)


def spread(row_mask, lane_hot, values):
    high, low = two_parts(values)
    left = jnp.concatenate([pick(row_mask, high.astype(F32)), pick(row_mask, low.astype(F32))], axis=1)
    right = jnp.concatenate([lane_hot, lane_hot], axis=1)
    return lax.dot_general(left, right, NT, preferred_element_type=F32)


def fetch_all(row_mask, lane_hot, fields):
    parts = [jnp.concatenate(two_parts(cells), axis=1) for cells in fields]
    wide = jnp.dot(
        jnp.concatenate(parts, axis=0), jnp.concatenate([lane_hot, lane_hot], axis=0), preferred_element_type=F32
    )
    count = row_mask.shape[0]
    return [
        jnp.sum(jnp.where(row_mask, wide[f * count : f * count + count], 0.0), axis=0, keepdims=True)
        for f in range(len(fields))
    ]


def as_lanes(row):
    return jnp.concatenate([row[:, a * 128 : (a + 1) * 128] for a in range(8)], axis=0)


def gather_body(
    stiff_ref, coef_ref, rows_ref, skin_ref, skin_prev_ref, mat_ref, str_ref, str_prev_ref, smat_ref,
    before_ref, after_ref, lefts_ref, rights_ref, later_ref,
    out_ref, ks_ref, ps_ref, cs_ref, kt_ref, pt_ref, ct_ref,
    half_ref, down_ref, across_ref, left_ref, thick_ref, edge_ref, tedge_ref, co_ref,
):
    tabs = tables(stiff_ref, coef_ref)
    (t_row, t_lane, tk), (s_row, s_lane, sk) = hots(rows_ref)
    ks_ref[...] = spread(s_row, s_lane, sk)
    kt_ref[...] = spread(t_row, t_lane, tk)
    edge_ref[...] = joined(lefts_ref[...], rights_ref[...])
    tedge_ref[...] = joined(before_ref[24:120, :], after_ref[24:120, :])
    bonds = (lambda l: down_ref, lambda l: across_ref, lambda l: left_ref, lambda l: thick_ref, lambda l: co_ref)

    def prepare(total, own, other, ends, edge, field):
        for r0 in range(0, total, CHUNK):
            sl = pl.ds(r0, CHUNK)
            half, coef = half_coef(own[sl, :], tabs)
            half_ref[sl, :] = half
            co_ref[sl, :] = coef
            thick_ref[sl, :] = 1.0 / (half + half_of(other[sl, :], tabs))
        layer_bonds(lambda lo, n: half_ref[pl.ds(lo, n), :], total, ends, edge, field, down_ref, across_ref, left_ref)

    prepare(128, mat_ref.at[1], mat_ref.at[0], ends_of(before_ref, after_ref, 23), edge_ref, 23)
    cs_ref[...] = co_ref[...]
    for r0 in range(0, 128, CHUNK):
        sl = pl.ds(r0, CHUNK)

        def put(c, value):
            ps_ref[c, sl, :] = value - cs_ref[sl, :] * ks_ref[sl, :] * skin_ref[c, 1, sl, :]

        chunk_step(
            lambda c, l: rows_of(skin_ref, c, l - 4), lambda c, l: rows_of(skin_prev_ref, c, 0), 128, r0, 5, 3, bonds,
            edge_ref, lambda c: c * 6 + 5, lambda c: ends_of(before_ref, after_ref, c * 6 + 5), None, put,
        )
    for p in range(2):
        prepare(96, smat_ref.at[p, 0], smat_ref.at[p, 1], None, tedge_ref, 36 + p * 6)
        lanes = pl.ds(p * 128, 128)
        ct_ref[:, p * 128 : p * 128 + 128] = co_ref[0:96, :]
        for r0 in range(0, 96, CHUNK):
            sl = pl.ds(r0, CHUNK)

            def put(c, value):
                pt_ref[c, sl, lanes] = value - ct_ref[sl, lanes] * kt_ref[sl, lanes] * str_ref[p, c, 0, sl, :]

            chunk_step(
                lambda c, l: rows_of(str_ref, p, c, l), lambda c, l: rows_of(str_prev_ref, p, c, l), 96, r0, 0, 3, bonds,
                tedge_ref, lambda c: (p * 3 + c) * 6, None, None, put,
            )
    t_fields = [jnp.concatenate([str_ref[0, c, 0], str_ref[1, c, 0]], axis=1) for c in range(3)]
    t_fields += [pt_ref[c] for c in range(3)] + [ct_ref[...] * kt_ref[...]]
    s_fields = [skin_ref[c, 1] for c in range(3)] + [ps_ref[c] for c in range(3)] + [cs_ref[...]]
    got = [as_lanes(row) for row in fetch_all(t_row, t_lane, t_fields) + fetch_all(s_row, s_lane, s_fields)]
    pad = jnp.zeros((8, 128), F32)
    got += [pad, pad]
    for j in range(4):
        part = [
            jnp.concatenate([g[:, q * 32 : q * 32 + 32] for g in got[4 * j : 4 * j + 4]], axis=1) for q in range(4)
        ]
        out_ref[pl.ds(j, 32, stride=4), :] = jnp.concatenate(part, axis=0)


def bounce_body(match_ref, got_ref, later_ref, out_ref):
    got = jnp.concatenate([got_ref[pl.ds(j, 32, stride=4), :] for j in range(4)], axis=1)
    lane = iota(got.shape, 1)
    zero = (lane & 16) == 0

    def turned(base):
        def part(to, frm):
            m = match_ref[base + to * 32 : base + to * 32 + 32, frm * 32 : frm * 32 + 32]
            return jnp.dot(m, got, preferred_element_type=F32, precision=lax.Precision.HIGHEST)

        a = part(0, 0) + pltpu.roll(part(0, 1), 512 - 16, 1)
        b = part(1, 1) + pltpu.roll(part(1, 0), 16, 1)
        return jnp.where(zero, a, b)

    new = jnp.where(lane < FIELDS * 32, turned(0), turned(64))
    for j in range(4):
        out_ref[pl.ds(j, 32, stride=4), :] = new[:, j * 128 : j * 128 + 128]


def spread_all(row_mask, lane_hot_t, values):
    rows = []
    for value in values:
        high, low = two_parts(value)
        rows.append(jnp.concatenate([pick(row_mask, high.astype(F32)), pick(row_mask, low.astype(F32))], axis=1))
    count = row_mask.shape[0]
    got = jnp.dot(
        jnp.concatenate(rows, axis=0), jnp.concatenate([lane_hot_t, lane_hot_t], axis=0), preferred_element_type=F32
    )
    return [got[f * count : f * count + count] for f in range(len(values))]


def load_body(
    rows_ref, posted_ref, ks_ref, ps_ref, cs_ref, kt_ref, pt_ref, ct_ref, skin_ref, str_ref,
    last_in, first_in, side_in, columns_in,
    skin1_ref, sload_ref, str1_ref, tload_ref, last_ref, first_ref, side_ref,
):
    (t_row, t_lane, tk), (s_row, s_lane, sk) = hots(rows_ref)
    posted = [posted_ref[pl.ds(j, 32, stride=4), :] for j in range(4)]

    def sums(side, row_mask, lane_hot, weight):
        values = []
        for f in range(FIELDS):
            g = side * FIELDS + f
            at = g % 4 * 32
            values.append(weight * one_row(row_lists(posted[g // 4][:, at : at + 32])))
        return spread_all(row_mask, lane_hot.astype(F32).T.astype(BF16), values)

    last_ref[0:24, :] = last_in[...]
    first_ref[0:24, :] = first_in[...]
    side = side_in[...]
    ks, cs = ks_ref[...], cs_ref[...]
    got = sums(0, s_row, s_lane, sk)
    for c in range(3):
        now = skin_ref[c, 0]
        new = ps_ref[c] + cs * got[c]
        skin1_ref[c] = new
        sload_ref[c] = got[3 + c] + got[6] * now - ks * new
        f = c * 6 + 5
        last_ref[f : f + 1, :] = new[127:128, :]
        first_ref[f : f + 1, :] = new[0:1, :]
        side = with_columns(side, new, f)
    side_ref[...] = side
    kt, ct = kt_ref[...], ct_ref[...]
    got = sums(1, t_row, t_lane, tk)
    third = iota((96, 256), 0) % 3
    columns = columns_in[...]
    for c in range(3):
        now = jnp.concatenate([str_ref[0, c, 0], str_ref[1, c, 0]], axis=1)
        own = kt * now
        pair = jnp.where(third == 0, pltpu.roll(own, 95, 0), jnp.where(third == 1, pltpu.roll(own, 1, 0), 0.0))
        new = pt_ref[c] + ct * got[c]
        load = got[3 + c] + got[6] * (own + pair) - kt * new
        for p in range(2):
            str1_ref[p, c] = new[:, p * 128 : p * 128 + 128]
            tload_ref[p, c] = load[:, p * 128 : p * 128 + 128]
            columns = with_columns(columns, new[:, p * 128 : p * 128 + 128], (p * 3 + c) * 6)
    last_ref[24:120, :] = columns
    first_ref[24:120, :] = columns


def bonds_body(
    stiff_ref, coef_ref, mat_ref, smat_ref, before_ref, after_ref, lefts_ref, rights_ref,
    sb_far, tb_far, sb_ref, tb_ref, sh_ref, th_ref, edge_ref, tedge_ref, sems,
):
    tabs = tables(stiff_ref, coef_ref)
    edge_ref[...] = joined(lefts_ref[...], rights_ref[...])
    tedge_ref[...] = joined(before_ref[24:120, :], after_ref[24:120, :])
    out = []

    def send(source, target):
        move = pltpu.make_async_copy(source, target, sems.at[len(out)])
        move.start()
        out.append(move)

    for l in range(6):
        for r0 in range(0, 128, CHUNK):
            sl = pl.ds(r0, CHUNK)
            half, coef = half_coef(mat_ref[l, sl, :], tabs)
            if l > 0:
                sb_ref[l - 1, 3, sl, :] = 1.0 / (half + sh_ref[l - 1, sl, :])
            sh_ref[l, sl, :] = half
            sb_ref[l, 4, sl, :] = coef
        layer_bonds(
            rows_of(sh_ref, l), 128, ends_of(before_ref, after_ref, 18 + l), edge_ref, 18 + l,
            sb_ref.at[l, 0], sb_ref.at[l, 1], sb_ref.at[l, 2],
        )
        if l > 0:
            send(sb_ref.at[l - 1], sb_far.at[l - 1])
    send(sb_ref.at[5], sb_far.at[5])
    for p in range(2):
        for t in range(6):
            for r0 in range(0, 96, CHUNK):
                sl = pl.ds(r0, CHUNK)
                half, coef = half_coef(smat_ref[p, t, sl, :], tabs)
                if t > 0:
                    tb_ref[p, t - 1, 3, sl, :] = 1.0 / (half + th_ref[t - 1, sl, :])
                th_ref[t, sl, :] = half
                tb_ref[p, t, 4, sl, :] = coef
            layer_bonds(
                rows_of(th_ref, t), 96, None, tedge_ref, 36 + p * 6 + t,
                tb_ref.at[p, t, 0], tb_ref.at[p, t, 1], tb_ref.at[p, t, 2],
            )
            if t > 0:
                send(tb_ref.at[p, t - 1], tb_far.at[p, t - 1])
        send(tb_ref.at[p, 5], tb_far.at[p, 5])
    finish(out)


def kinds(ref):
    return tuple((lambda l, k=k: ref.at[l, k]) for k in range(5))


def skin_layer(layer, now, prev, bonds, edge_ref, before_ref, after_ref, extra, put):
    for r0 in range(0, 128, CHUNK):
        chunk_step(
            now, prev, 128, r0, layer, 3, bonds, edge_ref, lambda c: c * 6 + layer,
            lambda c: ends_of(before_ref, after_ref, c * 6 + layer),
            None if extra is None else (lambda c: extra[c, pl.ds(r0, CHUNK), :]),
            lambda c, v: put(c, pl.ds(r0, CHUNK), v),
        )


def str_layer(p, layer, now, prev, bonds, edge_ref, extra, put):
    for r0 in range(0, 96, CHUNK):
        chunk_step(
            now, prev, 96, r0, layer, 3, bonds, edge_ref, lambda c: (p * 3 + c) * 6 + layer, None,
            None if extra is None else (lambda c: extra[p, c, pl.ds(r0, CHUNK), :]),
            lambda c, v: put(c, pl.ds(r0, CHUNK), v),
        )


def moving(pairs, sems):
    moves = {}
    for key, source, target in pairs:
        moves[key] = pltpu.make_async_copy(source, target, sems.at[len(moves)])
        moves[key].start()
    return moves


def first_skin_body(
    skin_far, prev_far, before_far, after_far, lefts_far, rights_far, sb_far, later_ref,
    skin1_far, last_ref, first_ref, side_ref,
    skin_ref, prev_ref, before_ref, after_ref, lefts_ref, rights_ref, sb_ref, skin1_ref, edge_ref, sems,
):
    pairs = [
        ("l", lefts_far, lefts_ref), ("r", rights_far, rights_ref), ("b", before_far, before_ref), ("a", after_far, after_ref),
    ]
    for l in range(6):
        pairs.append((("u", l), skin_far.at[:, l], skin_ref.at[:, l]))
        if l < 5:
            pairs += [(("k", l), sb_far.at[l], sb_ref.at[l]), (("v", l), prev_far.at[:, l], prev_ref.at[:, l])]
    moves = moving(pairs, sems)
    need = gate(moves)
    last_ref[...] = jnp.zeros((24, 128), F32)
    first_ref[...] = jnp.zeros((24, 128), F32)
    need("l", "r", "b", "a")
    edge_ref[...] = joined(lefts_ref[...], rights_ref[...])
    out = []
    for l in range(5):
        need(("u", l), ("u", l + 1), ("k", l), ("v", l))

        def put(c, sl, value):
            skin1_ref[c, l, sl, :] = value

        skin_layer(
            l, lambda c, m: rows_of(skin_ref, c, m), lambda c, m: rows_of(prev_ref, c, m), kinds(sb_ref), edge_ref,
            before_ref, after_ref, None, put,
        )
        out.append(pltpu.make_async_copy(skin1_ref.at[:, l], skin1_far.at[:, l], sems.at[len(pairs) + l]))
        out[l].start()
    for r0 in range(0, 128, CHUNK):
        side_ref[pl.ds(r0, CHUNK), :] = pack_skin(
            jnp.zeros((CHUNK, 128), F32), lambda c, l: skin1_ref[c, l, pl.ds(r0, CHUNK), :], range(5), r0, first_ref, last_ref
        )
    finish(out)


def first_str_body(
    str_far, prev_far, before_far, after_far, tb_far, later_ref,
    str1_far, columns_ref,
    str_ref, prev_ref, before_ref, after_ref, tb_ref, str1_ref, tedge_ref, sems,
):
    pairs = [("b", before_far, before_ref), ("a", after_far, after_ref)]
    for p in range(2):
        for t in range(6):
            pairs += [
                (("u", p, t), str_far.at[p, :, t], str_ref.at[p, :, t]), (("k", p, t), tb_far.at[p, t], tb_ref.at[p, t]),
            ]
            if t > 0:
                pairs.append((("v", p, t), prev_far.at[p, :, t], prev_ref.at[p, :, t]))
    moves = moving(pairs, sems)
    need = gate(moves)
    need("b", "a")
    tedge_ref[...] = joined(before_ref[24:120, :], after_ref[24:120, :])
    out = []
    for p in range(2):
        for t in range(1, 6):
            need(("u", p, t - 1), ("k", p, t - 1), ("u", p, t), ("u", p, t + 1), ("k", p, t), ("v", p, t))

            def put(c, sl, value):
                str1_ref[p, c, t - 1, sl, :] = value

            str_layer(
                p, t, lambda c, m: rows_of(str_ref, p, c, m), lambda c, m: rows_of(prev_ref, p, c, m),
                kinds(tb_ref.at[p]), tedge_ref, None, put,
            )
            move = pltpu.make_async_copy(
                str1_ref.at[p, :, t - 1], str1_far.at[p, :, t - 1], sems.at[len(pairs) + len(out)]
            )
            move.start()
            out.append(move)
    for r0 in range(0, 96, CHUNK):
        columns_ref[pl.ds(r0, CHUNK), :] = pack_str(
            jnp.zeros((CHUNK, 128), F32), lambda p, c, t: str1_ref[p, c, t - 1, pl.ds(r0, CHUNK), :], range(1, 6)
        )
    finish(out)


def second_body(
    skin_far, prev_far, str_far, str_prev_far, before_far, after_far, lefts_far, rights_far, sb_far, tb_far,
    skin_face_far, str_face_far, sload_far, tload_far,
    skin2_far, str2_far,
    skin_ref, prev_ref, str_ref, str_prev_ref, before_ref, after_ref, lefts_ref, rights_ref, sb_ref, tb_ref,
    skin_face_ref, str_face_ref, sload_ref, tload_ref,
    skin2_ref, str2_ref, edge_ref, tedge_ref, sems,
):
    pairs = [
        ("l", lefts_far, lefts_ref), ("r", rights_far, rights_ref), ("b", before_far, before_ref), ("a", after_far, after_ref),
    ]
    for l in range(6):
        if l < 5:
            pairs.append((("u", l), skin_far.at[:, l], skin_ref.at[:, l]))
        else:
            pairs += [(("u", l), skin_face_far, skin_face_ref), ("s", sload_far, sload_ref)]
        pairs += [(("k", l), sb_far.at[l], sb_ref.at[l]), (("v", l), prev_far.at[:, l], prev_ref.at[:, l])]
    pairs += [("f", str_face_far, str_face_ref), ("t", tload_far, tload_ref)]
    for p in range(2):
        for t in range(6):
            if t > 0:
                pairs.append((("u", p, t), str_far.at[p, :, t - 1], str_ref.at[p, :, t - 1]))
            pairs += [
                (("k", p, t), tb_far.at[p, t], tb_ref.at[p, t]),
                (("v", p, t), str_prev_far.at[p, :, t], str_prev_ref.at[p, :, t]),
            ]
    moves = moving(pairs, sems)
    need = gate(moves)
    need("l", "r", "b", "a")
    edge_ref[...] = joined(lefts_ref[...], rights_ref[...])
    tedge_ref[...] = joined(before_ref[24:120, :], after_ref[24:120, :])
    out = []

    def send(source, target):
        move = pltpu.make_async_copy(source, target, sems.at[len(pairs) + len(out)])
        move.start()
        out.append(move)

    for l in range(6):
        need(("u", l), ("u", l + 1), ("k", l), ("v", l))
        if l == 5:
            need("s")

        def put(c, sl, value):
            skin2_ref[c, l, sl, :] = value

        skin_layer(
            l, lambda c, m: rows_of(skin_face_ref, c) if m == 5 else rows_of(skin_ref, c, m),
            lambda c, m: rows_of(prev_ref, c, m), kinds(sb_ref), edge_ref, before_ref, after_ref,
            sload_ref if l == 5 else None, put,
        )
        send(skin2_ref.at[:, l], skin2_far.at[:, l])
    need("f", "t")
    for p in range(2):
        for t in range(6):
            need(("u", p, t), ("u", p, t + 1), ("k", p, t), ("v", p, t))

            def put(c, sl, value):
                str2_ref[p, c, t, sl, :] = value

            str_layer(
                p, t, lambda c, m: rows_of(str_face_ref, p, c) if m == 0 else rows_of(str_ref, p, c, m - 1),
                lambda c, m: rows_of(str_prev_ref, p, c, m), kinds(tb_ref.at[p]), tedge_ref,
                tload_ref if t == 0 else None, put,
            )
            send(str2_ref.at[p, :, t], str2_far.at[p, :, t])
    finish(out)


def swap(values):
    peers = lax.axis_size("chord")
    moved = lax.all_to_all(values.reshape(peers, -1, 128), "chord", split_axis=0, concat_axis=0, tiled=True)
    return moved.reshape(values.shape)


def shards(
    skin_now, skin_prev, skin_mat, stringer_now, stringer_prev, stringer_mat, owner_slot,
    rivet_span, rivet_chord, rivet_stringer, rivet_cell, rivet_stiff, mat_stiff, mat_coef,
):
    mats = [mat_stiff, mat_coef]
    own = [skin_now, skin_mat, stringer_now, stringer_mat]
    column = [(120, 128), (120, 128), (128, 128)]
    sent, match, *packs = call(
        opening_body, [(32, 128), (128, 128), *column],
        [*mats, rivet_span, rivet_chord, rivet_stringer, rivet_cell, rivet_stiff, owner_slot.reshape(1, -1), *own],
        "opening", smem=(0, 1), far=range(8, 12), flops=4000000, nbytes=4000000, scratch=near(own), sems=4,
    )
    rows = swap(sent)
    halos = exchange(*packs)
    edges = [(128, 128), (96, 128)]
    bonds = [(6, 5, 136, 128), (2, 6, 5, 104, 128)]
    bonds = call(
        bonds_body, bonds, [*mats, skin_mat, stringer_mat, *halos], "bonds", smem=(0, 1), far_outs=(0, 1),
        flops=10000000, nbytes=8000000, scratch=floats(*bonds, (6, 128, 128), (6, 96, 128), *edges), sems=18,
    )
    found, *kept = call(
        gather_body, [(128, 128), (128, 128), (3, 128, 128), (128, 128), (96, 256), (3, 96, 256), (96, 256)],
        [*mats, rows, skin_now, skin_prev, skin_mat, stringer_now, stringer_prev, stringer_mat, *halos, bonds[0]], "gather",
        smem=(0, 1), far=(13,), flops=1000000000, nbytes=2000000,
        views={
            3: ((3, 2, 128, 128), (0, 2, 0, 0)),
            4: ((3, 1, 128, 128), (0, 5, 0, 0)),
            5: ((2, 128, 128), (2, 0, 0)),
            6: ((2, 3, 2, 96, 128), (0, 0, 0, 0, 0)),
            7: ((2, 3, 1, 96, 128), (0, 0, 0, 0, 0)),
            8: ((2, 2, 96, 128), (0, 0, 0, 0)),
        },
        scratch=floats((128, 128), (136, 128), (128, 128), (128, 128), (128, 128), *edges, (128, 128)),
    )
    given = swap(found)
    parts = [skin_now, skin_prev, *halos, bonds[0]]
    skin1, last, first, side = call(
        first_skin_body, [(3, 5, 128, 128), (24, 128), (24, 128), (128, 128)], [*parts, found], "first_skin",
        far=range(8), far_outs=(0,), flops=10000000, nbytes=5000000,
        scratch=near(parts) + floats((3, 5, 128, 128), (128, 128)), sems=25,
    )
    (turned,) = call(bounce_body, [(128, 128)], [match, given, last], "bounce", fast=(1,), far=(2,), limit=8)
    posted = swap(turned)
    parts = [stringer_now, stringer_prev, *halos[:2], bonds[1]]
    str1, columns = call(
        first_str_body, [(2, 3, 5, 96, 128), (96, 128)], [*parts, turned], "first_str",
        far=range(6), far_outs=(0,), flops=10000000, nbytes=5000000,
        scratch=near(parts) + floats((2, 3, 5, 96, 128), (96, 128)), sems=46,
    )
    skin_face, sload, str_face, tload, *packs2 = call(
        load_body, [(3, 128, 128), (3, 128, 128), (2, 3, 96, 128), (2, 3, 96, 128), *column],
        [rows, posted, *kept, skin_now, stringer_now, last, first, side, columns], "load", flops=1000000000, nbytes=2000000,
        views={8: ((3, 1, 128, 128), (0, 5, 0, 0)), 9: ((2, 3, 1, 96, 128), (0, 0, 0, 0, 0))},
    )
    halos1 = exchange(*packs2)
    parts = [skin1, skin_now, str1, stringer_now, *halos1, *bonds, skin_face, str_face, sload, tload]
    results = [(3, 6, 128, 128), (2, 3, 6, 96, 128)]
    return call(
        second_body, results, parts, "second", far=range(14), far_outs=(0, 1), flops=20000000, nbytes=10000000,
        scratch=near(parts) + floats(*results, *edges), sems=80, limit=56,
    )


def solution(mesh):
    placed = (
        P(None, None, "span", "chord"),
        P(None, None, "span", "chord"),
        P(None, "span", "chord"),
        P("chord", None, None, None, "span"),
        P("chord", None, None, None, "span"),
        P("chord", None, None, "span"),
        P(),
        P(("span", "chord")),
        P(("span", "chord")),
        P(("span", "chord")),
        P(("span", "chord")),
        P(("span", "chord")),
        P(),
        P(),
    )
    body = jax.shard_map(
        shards,
        mesh=mesh,
        in_specs=placed,
        out_specs=(P(None, None, "span", "chord"), P("chord", None, None, None, "span")),
        check_vma=False,
    )
    return lambda *args: tuple(body(*args))
```

```python
import jax
import jax.numpy as jnp
from jax import lax
from jax.experimental import pallas as pl
from jax.experimental.pallas import tpu as pltpu
from jax.sharding import PartitionSpec as P

F32 = jnp.float32
BF16 = jnp.bfloat16
NT = (((1,), (1,)), ((), ()))
TN = (((0,), (0,)), ((), ()))
FIELDS = 7


def iota(shape, dim):
    return lax.broadcasted_iota(jnp.int32, shape, dim)


def two_parts(values):
    high = values.astype(BF16)
    return high, (values - high.astype(F32)).astype(BF16)


def pick(mask, values):
    return jnp.where(mask, values, 0.0).astype(BF16)


def whole(shape):
    return pl.BlockSpec(tuple(shape), lambda i: (0,) * len(shape), pipeline_mode=pl.Buffered(1))


def call(body, outs, ins, name, smem=(), far=(), fast=(), views=None, far_outs=(), flops=0, nbytes=0, scratch=(), sems=0, limit=56):
    views = views or {}

    def spec(i, a):
        if i in smem:
            return pl.BlockSpec(memory_space=pltpu.SMEM)
        if i in far:
            return pl.BlockSpec(memory_space=pl.ANY)
        if i in fast:
            return pl.BlockSpec(memory_space=pltpu.VMEM)
        if i in views:
            shape, at = views[i]
            return pl.BlockSpec(shape, lambda g: at)
        return whole(a.shape)

    return pl.pallas_call(
        body,
        grid=(1,),
        out_shape=[jax.ShapeDtypeStruct(s, F32) for s in outs],
        in_specs=[spec(i, a) for i, a in enumerate(ins)],
        out_specs=[pl.BlockSpec(memory_space=pl.ANY) if i in far_outs else whole(s) for i, s in enumerate(outs)],
        scratch_shapes=[pltpu.VMEM(s, t) for s, t in scratch] + ([pltpu.SemaphoreType.DMA((sems,))] if sems else []),
        compiler_params=pltpu.CompilerParams(vmem_limit_bytes=limit * 1024 * 1024),
        cost_estimate=pl.CostEstimate(flops=flops, bytes_accessed=nbytes, transcendentals=0),
        name=name,
    )(*ins)


def gate(moves):
    waited = set()

    def need(*keys):
        for key in keys:
            if key in moves and key not in waited:
                waited.add(key)
                moves[key].wait()

    return need


def near(arrays):
    return [(a.shape, a.dtype) for a in arrays]


def floats(*shapes):
    return [(s, F32) for s in shapes]


def copies(sources, targets, sems, at=0):
    return [pltpu.make_async_copy(s, t, sems.at[at + i]) for i, (s, t) in enumerate(zip(sources, targets))]


def start(moves):
    for move in moves:
        move.start()


def finish(moves):
    for move in moves:
        move.wait()


def tables(stiff_ref, coef_ref):
    half = [0.5 / jnp.full((1, 128), stiff_ref[m], F32) for m in range(8)]
    return half, [coef_ref[m] for m in range(8)]


def half_of(mat, tabs):
    out = jnp.broadcast_to(tabs[0][0], mat.shape)
    for m in range(1, 8):
        out = jnp.where(mat == m, tabs[0][m], out)
    return out


def half_coef(mat, tabs):
    half = jnp.broadcast_to(tabs[0][0], mat.shape)
    coef = jnp.full(mat.shape, tabs[1][0], F32)
    for m in range(1, 8):
        same = mat == m
        half = jnp.where(same, tabs[0][m], half)
        coef = jnp.where(same, tabs[1][m], coef)
    return half, coef


CHUNK = 32


def joined(before, after):
    lane = iota(before.shape, 1)
    return jnp.where((lane & 1) == 1, pltpu.roll(before, 1, 1), pltpu.roll(after, 127, 1))


def with_columns(columns, cells, field):
    lane = iota(cells.shape, 1)
    return jnp.where((lane >> 1) == field, pltpu.roll(cells, 2 * field + 1, 1), columns)


def row_neighbours(get, r0, total, ends):
    cells = get(r0, CHUNK)
    row = iota(cells.shape, 0)
    if r0 > 0:
        above = get(r0 - 1, CHUNK)
    else:
        above = pltpu.roll(cells, 1, 0)
        if ends is not None:
            above = jnp.where(row == 0, ends[0], above)
    if r0 + CHUNK < total:
        below = get(r0 + 1, CHUNK)
    else:
        below = pltpu.roll(cells, CHUNK - 1, 0)
        if ends is not None:
            below = jnp.where(row == CHUNK - 1, ends[1], below)
    return cells, above, below


def lane_neighbours(cells, edge, field):
    lane = iota(cells.shape, 1)
    turned = pltpu.roll(edge, (127 - 2 * field) % 128, 1)
    before = jnp.where(lane == 0, turned, pltpu.roll(cells, 1, 1))
    after = jnp.where(lane == 127, turned, pltpu.roll(cells, 127, 1))
    return before, after


def safe_bond(half, beside):
    return jnp.where(beside > 0.0, 1.0 / (half + beside), 0.0)


def layer_bonds(get, total, ends, edge, field, down, across, left):
    for r0 in range(0, total, CHUNK):
        half, _, below = row_neighbours(get, r0, total, ends)
        bond = safe_bond(half, below)
        if ends is None and r0 + CHUNK == total:
            bond = jnp.where(iota(half.shape, 0) == CHUNK - 1, 0.0, bond)
        down[8 + r0 : 8 + r0 + CHUNK, :] = bond
        if r0 == 0:
            down[7:8, :] = jnp.zeros((1, 128), F32) if ends is None else safe_bond(half[0:1], ends[0])
        before, after = lane_neighbours(half, edge[r0 : r0 + CHUNK, :], field)
        left[r0 : r0 + CHUNK, :] = safe_bond(half, before)
        across[r0 : r0 + CHUNK, :] = safe_bond(half, after)


def chunk_step(now, prev, total, r0, layer, comps, bonds, edge, fields, ends, extra, put):
    down, across, left, thick, coef = bonds
    sl = pl.ds(r0, CHUNK)
    up = down(layer)[pl.ds(7 + r0, CHUNK), :]
    dn = down(layer)[pl.ds(8 + r0, CHUNK), :]
    ac, al, co = across(layer)[sl, :], left(layer)[sl, :], coef(layer)[sl, :]
    for c in range(comps):
        cells, above, below = row_neighbours(now(c, layer), r0, total, None if ends is None else ends(c))
        before, after = lane_neighbours(cells, edge[sl, :], fields(c))
        pull = dn * (below - cells) + up * (above - cells)
        pull = pull + (ac * (after - cells) + al * (before - cells))
        if layer < 5:
            pull = pull + thick(layer)[sl, :] * (now(c, layer + 1)(r0, CHUNK) - cells)
        if layer > 0:
            pull = pull + thick(layer - 1)[sl, :] * (now(c, layer - 1)(r0, CHUNK) - cells)
        if extra is not None:
            pull = pull + extra(c)
        put(c, 2.0 * cells - prev(c, layer)(r0, CHUNK) + co * pull)


def rows_of(ref, *index):
    view = ref.at[index]
    return lambda lo, n: view[pl.ds(lo, n), :]


def ends_of(before, after, index):
    return before[index : index + 1, :], after[index : index + 1, :]


def prep_part(span_ref, chord_ref, stringer_ref, cell_ref, stiff_ref, owner_ref, out_ref, match_ref):
    def row_of(ref):
        return ref[...].reshape(1, -1)

    span, chord, stringer = row_of(span_ref), row_of(chord_ref), row_of(stringer_ref)
    cell, stiff = row_of(cell_ref), row_of(stiff_ref)
    count = span.shape[1]
    chunks = count // 128
    same = iota((48, count), 0) == stringer
    diagonal = iota((48, 48), 0) == iota((48, 48), 1)
    owner = jnp.sum(jnp.where(diagonal, owner_ref[...], 0).astype(F32), axis=1, keepdims=True).astype(jnp.int32)
    slot = jnp.sum(jnp.where(same, owner, 0).astype(F32), axis=0, keepdims=True).astype(jnp.int32)
    foot = (chord - (((2 * cell) * 171) >> 9)) >> 6
    foot_of = jnp.max(jnp.where(same, foot, 0).astype(F32), axis=1, keepdims=True).astype(jnp.int32)
    slots = iota((48, 64), 1)
    slot_hot = (slots == (owner & 1) * 32 + (owner >> 1)).astype(F32).astype(BF16)
    foot_hot = (slots == (foot_of & 1) * 32 + (foot_of >> 1)).astype(F32).astype(BF16)
    match_ref[0:64, 0:64] = lax.dot_general(foot_hot, slot_hot, TN, preferred_element_type=F32)
    match_ref[64:128, 0:64] = lax.dot_general(slot_hot, foot_hot, TN, preferred_element_type=F32)
    one = same.astype(F32)
    lower = (iota((128, 128), 0) < iota((128, 128), 1)).astype(F32).astype(BF16)
    both = jnp.concatenate([lower, jnp.ones((128, 128), BF16)], axis=1)
    offset = jnp.zeros((48, 128), F32)
    ranks = []
    for k in range(chunks):
        part = one[:, k * 128 : (k + 1) * 128]
        ahead = jnp.dot(part.astype(BF16), both, preferred_element_type=F32)
        ranks.append(jnp.sum(part * (ahead[:, :128] + offset), axis=0, keepdims=True))
        offset = offset + ahead[:, 128:]
    rank = jnp.concatenate(ranks, axis=1).astype(jnp.int32)
    place = iota((128, count), 0)
    place = place == jnp.where(
        place < 64, (slot & 1) * 32 + (slot >> 1), 64 + (foot & 1) * 32 + (foot >> 1)
    )
    place = place.astype(F32).astype(BF16)
    order = iota((16, count), 0) == rank
    high = stiff.astype(BF16).astype(F32)
    rest = stiff - high
    middle = rest.astype(BF16).astype(F32)
    fields = [cell.astype(F32), (span & 127).astype(F32), (chord & 127).astype(F32), high, middle, rest - middle]
    rows = jnp.concatenate([pick(order, f) for f in fields], axis=0)
    got = lax.dot_general(place, rows, NT, preferred_element_type=F32)
    for side in range(2):
        index, weight = [], []
        for p in range(2):
            part = got[side * 64 + p * 32 : side * 64 + p * 32 + 32]
            where_, across = part[:, 0:16], part[:, 16:32]
            if side == 1:
                where_, across = part[:, 16:32], part[:, 32:48]
            index.append(where_ * 128.0 + across)
            weight.append(part[:, 48:64] + part[:, 64:80] + part[:, 80:96])
        out_ref[:, side * 64 : side * 64 + 64] = jnp.concatenate(index + weight, axis=1)


def ends_exist():
    span, chord = lax.axis_index("span"), lax.axis_index("chord")
    yes = lambda cond: jnp.where(cond, 1.0, 0.0).astype(F32)
    return (
        yes(span > 0), yes(span < lax.axis_size("span") - 1),
        yes(chord > 0), yes(chord < lax.axis_size("chord") - 1),
    )


def pack_skin(columns, get, layers, r0, first_ref, last_ref):
    for l in layers:
        for c in range(3):
            f = c * 6 + l
            cells = get(c, l)
            columns = with_columns(columns, cells, f)
            if r0 == 0:
                first_ref[f : f + 1, :] = cells[0:1]
            if r0 == 128 - CHUNK:
                last_ref[f : f + 1, :] = cells[CHUNK - 1 : CHUNK]
    return columns


def pack_str(columns, get, layers):
    for p in range(2):
        for t in layers:
            for c in range(3):
                columns = with_columns(columns, get(p, c, t), (p * 3 + c) * 6 + t)
    return columns


def halo_part(stiff_ref, coef_ref, skin_ref, mat_ref, str_ref, smat_ref, last_ref, first_ref, side_ref):
    tabs = tables(stiff_ref, coef_ref)
    at_prev, at_next, at_left, at_right = ends_exist()
    lane = iota((CHUNK, 128), 1)
    side_keep = jnp.where((lane & 1) == 0, at_right, at_left)
    span_keep = jnp.where((lane & 1) == 0, at_next, at_prev)
    for l in range(6):
        first_ref[18 + l : 19 + l, :] = half_of(mat_ref[l, 0:1, :], tabs) * at_prev
        last_ref[18 + l : 19 + l, :] = half_of(mat_ref[l, 127:128, :], tabs) * at_next
    for r0 in range(0, 128, CHUNK):
        mats = jnp.zeros((CHUNK, 128), jnp.int32)
        for l in range(6):
            mats = with_columns(mats, mat_ref[l, pl.ds(r0, CHUNK), :], 18 + l)
        columns = jnp.where(((lane >> 1) >= 18) & ((lane >> 1) < 24), half_of(mats, tabs) * side_keep, 0.0)
        side_ref[pl.ds(r0, CHUNK), :] = pack_skin(
            columns, lambda c, l: skin_ref[c, l, pl.ds(r0, CHUNK), :], range(6), r0, first_ref, last_ref
        )
    for r0 in range(0, 96, CHUNK):
        mats = jnp.zeros((CHUNK, 128), jnp.int32)
        for p in range(2):
            for t in range(6):
                mats = with_columns(mats, smat_ref[p, t, pl.ds(r0, CHUNK), :], 36 + p * 6 + t)
        columns = jnp.where(((lane >> 1) >= 36) & ((lane >> 1) < 48), half_of(mats, tabs) * span_keep, 0.0)
        columns = pack_str(columns, lambda p, c, t: str_ref[p, c, t, pl.ds(r0, CHUNK), :], range(6))
        last_ref[pl.ds(24 + r0, CHUNK), :] = columns
        first_ref[pl.ds(24 + r0, CHUNK), :] = columns


def opening_body(
    stiff_ref, coef_ref, span_ref, chord_ref, stringer_ref, cell_ref, weight_ref, owner_ref,
    skin_far, mat_far, str_far, smat_far,
    sent_ref, match_ref, last_ref, first_ref, side_ref,
    skin_ref, mat_ref, str_ref, smat_ref, sems,
):
    moves = copies([skin_far, mat_far, str_far, smat_far], [skin_ref, mat_ref, str_ref, smat_ref], sems)
    start(moves)
    prep_part(span_ref, chord_ref, stringer_ref, cell_ref, weight_ref, owner_ref, sent_ref, match_ref)
    finish(moves)
    halo_part(stiff_ref, coef_ref, skin_ref, mat_ref, str_ref, smat_ref, last_ref, first_ref, side_ref)


def exchange(last, first, side):
    def ring(axis):
        count = lax.axis_size(axis)
        return [(i, (i + 1) % count) for i in range(count)]

    back = lambda pairs: [(b, a) for a, b in pairs]
    lefts = lax.ppermute(side, "chord", ring("chord"))
    rights = lax.ppermute(side, "chord", back(ring("chord")))
    before = lax.ppermute(last, "span", ring("span"))
    after = lax.ppermute(first, "span", back(ring("span")))
    return before, after, lefts, rights


def row_lists(index):
    return jnp.concatenate([index[q * 8 : q * 8 + 8, :] for q in range(4)], axis=1)


def one_row(values):
    return jnp.concatenate([values[a : a + 1, :] for a in range(8)], axis=1)


def hots(rows_ref):
    text = one_row(row_lists(rows_ref[:, 0:32])).astype(jnp.int32)
    tk = one_row(row_lists(rows_ref[:, 32:64]))
    sext = one_row(row_lists(rows_ref[:, 64:96])).astype(jnp.int32)
    sk = one_row(row_lists(rows_ref[:, 96:128]))
    slot = ((iota((1, 1024), 1) >> 4) & 1) * 128
    t_row = iota((96, 1024), 0) == (text >> 7)
    t_lane = (iota((256, 1024), 0) == (text & 127) + slot).astype(F32).astype(BF16)
    s_row = iota((128, 1024), 0) == (sext >> 7)
    s_lane = (iota((128, 1024), 0) == (sext & 127)).astype(F32).astype(BF16)
    return (t_row, t_lane, tk), (s_row, s_lane, sk)


def spread(row_mask, lane_hot, values):
    high, low = two_parts(values)
    left = jnp.concatenate([pick(row_mask, high.astype(F32)), pick(row_mask, low.astype(F32))], axis=1)
    right = jnp.concatenate([lane_hot, lane_hot], axis=1)
    return lax.dot_general(left, right, NT, preferred_element_type=F32)


def fetch_all(row_mask, lane_hot, fields):
    parts = [jnp.concatenate(two_parts(cells), axis=1) for cells in fields]
    wide = jnp.dot(
        jnp.concatenate(parts, axis=0), jnp.concatenate([lane_hot, lane_hot], axis=0), preferred_element_type=F32
    )
    count = row_mask.shape[0]
    return [
        jnp.sum(jnp.where(row_mask, wide[f * count : f * count + count], 0.0), axis=0, keepdims=True)
        for f in range(len(fields))
    ]


def as_lanes(row):
    return jnp.concatenate([row[:, a * 128 : (a + 1) * 128] for a in range(8)], axis=0)


def gather_body(
    stiff_ref, coef_ref, rows_ref, skin_ref, skin_prev_ref, mat_ref, str_ref, str_prev_ref, smat_ref,
    before_ref, after_ref, lefts_ref, rights_ref, later_ref,
    out_ref, ks_ref, ps_ref, cs_ref, kt_ref, pt_ref, ct_ref,
    half_ref, down_ref, across_ref, left_ref, thick_ref, edge_ref, tedge_ref, co_ref,
):
    tabs = tables(stiff_ref, coef_ref)
    (t_row, t_lane, tk), (s_row, s_lane, sk) = hots(rows_ref)
    ks_ref[...] = spread(s_row, s_lane, sk)
    kt_ref[...] = spread(t_row, t_lane, tk)
    edge_ref[...] = joined(lefts_ref[...], rights_ref[...])
    tedge_ref[...] = joined(before_ref[24:120, :], after_ref[24:120, :])
    bonds = (lambda l: down_ref, lambda l: across_ref, lambda l: left_ref, lambda l: thick_ref, lambda l: co_ref)

    def prepare(total, own, other, ends, edge, field):
        for r0 in range(0, total, CHUNK):
            sl = pl.ds(r0, CHUNK)
            half, coef = half_coef(own[sl, :], tabs)
            half_ref[sl, :] = half
            co_ref[sl, :] = coef
            thick_ref[sl, :] = 1.0 / (half + half_of(other[sl, :], tabs))
        layer_bonds(lambda lo, n: half_ref[pl.ds(lo, n), :], total, ends, edge, field, down_ref, across_ref, left_ref)

    prepare(128, mat_ref.at[1], mat_ref.at[0], ends_of(before_ref, after_ref, 23), edge_ref, 23)
    cs_ref[...] = co_ref[...]
    for r0 in range(0, 128, CHUNK):
        sl = pl.ds(r0, CHUNK)

        def put(c, value):
            ps_ref[c, sl, :] = value - cs_ref[sl, :] * ks_ref[sl, :] * skin_ref[c, 1, sl, :]

        chunk_step(
            lambda c, l: rows_of(skin_ref, c, l - 4), lambda c, l: rows_of(skin_prev_ref, c, 0), 128, r0, 5, 3, bonds,
            edge_ref, lambda c: c * 6 + 5, lambda c: ends_of(before_ref, after_ref, c * 6 + 5), None, put,
        )
    for p in range(2):
        prepare(96, smat_ref.at[p, 0], smat_ref.at[p, 1], None, tedge_ref, 36 + p * 6)
        lanes = pl.ds(p * 128, 128)
        ct_ref[:, p * 128 : p * 128 + 128] = co_ref[0:96, :]
        for r0 in range(0, 96, CHUNK):
            sl = pl.ds(r0, CHUNK)

            def put(c, value):
                pt_ref[c, sl, lanes] = value - ct_ref[sl, lanes] * kt_ref[sl, lanes] * str_ref[p, c, 0, sl, :]

            chunk_step(
                lambda c, l: rows_of(str_ref, p, c, l), lambda c, l: rows_of(str_prev_ref, p, c, l), 96, r0, 0, 3, bonds,
                tedge_ref, lambda c: (p * 3 + c) * 6, None, None, put,
            )
    t_fields = [jnp.concatenate([str_ref[0, c, 0], str_ref[1, c, 0]], axis=1) for c in range(3)]
    t_fields += [pt_ref[c] for c in range(3)] + [ct_ref[...] * kt_ref[...]]
    s_fields = [skin_ref[c, 1] for c in range(3)] + [ps_ref[c] for c in range(3)] + [cs_ref[...]]
    got = [as_lanes(row) for row in fetch_all(t_row, t_lane, t_fields) + fetch_all(s_row, s_lane, s_fields)]
    pad = jnp.zeros((8, 128), F32)
    got += [pad, pad]
    for j in range(4):
        part = [
            jnp.concatenate([g[:, q * 32 : q * 32 + 32] for g in got[4 * j : 4 * j + 4]], axis=1) for q in range(4)
        ]
        out_ref[pl.ds(j, 32, stride=4), :] = jnp.concatenate(part, axis=0)


def bounce_body(match_ref, got_ref, out_ref):
    got = jnp.concatenate([got_ref[pl.ds(j, 32, stride=4), :] for j in range(4)], axis=1)
    lane = iota(got.shape, 1)
    zero = (lane & 16) == 0

    def turned(base):
        def part(to, frm):
            m = match_ref[base + to * 32 : base + to * 32 + 32, frm * 32 : frm * 32 + 32]
            return jnp.dot(m, got, preferred_element_type=F32, precision=lax.Precision.HIGHEST)

        a = part(0, 0) + pltpu.roll(part(0, 1), 512 - 16, 1)
        b = part(1, 1) + pltpu.roll(part(1, 0), 16, 1)
        return jnp.where(zero, a, b)

    new = jnp.where(lane < FIELDS * 32, turned(0), turned(64))
    for j in range(4):
        out_ref[pl.ds(j, 32, stride=4), :] = new[:, j * 128 : j * 128 + 128]


def spread_all(row_mask, lane_hot_t, values):
    rows = []
    for value in values:
        high, low = two_parts(value)
        rows.append(jnp.concatenate([pick(row_mask, high.astype(F32)), pick(row_mask, low.astype(F32))], axis=1))
    count = row_mask.shape[0]
    got = jnp.dot(
        jnp.concatenate(rows, axis=0), jnp.concatenate([lane_hot_t, lane_hot_t], axis=0), preferred_element_type=F32
    )
    return [got[f * count : f * count + count] for f in range(len(values))]


def load_body(
    rows_ref, posted_ref, ks_ref, ps_ref, cs_ref, kt_ref, pt_ref, ct_ref, skin_ref, str_ref,
    last_in, first_in, side_in, columns_in,
    skin1_ref, sload_ref, str1_ref, tload_ref, last_ref, first_ref, side_ref,
):
    (t_row, t_lane, tk), (s_row, s_lane, sk) = hots(rows_ref)
    posted = [posted_ref[pl.ds(j, 32, stride=4), :] for j in range(4)]

    def sums(side, row_mask, lane_hot, weight):
        values = []
        for f in range(FIELDS):
            g = side * FIELDS + f
            at = g % 4 * 32
            values.append(weight * one_row(row_lists(posted[g // 4][:, at : at + 32])))
        return spread_all(row_mask, lane_hot.astype(F32).T.astype(BF16), values)

    last_ref[0:24, :] = last_in[...]
    first_ref[0:24, :] = first_in[...]
    side = side_in[...]
    ks, cs = ks_ref[...], cs_ref[...]
    got = sums(0, s_row, s_lane, sk)
    for c in range(3):
        now = skin_ref[c, 0]
        new = ps_ref[c] + cs * got[c]
        skin1_ref[c] = new
        sload_ref[c] = got[3 + c] + got[6] * now - ks * new
        f = c * 6 + 5
        last_ref[f : f + 1, :] = new[127:128, :]
        first_ref[f : f + 1, :] = new[0:1, :]
        side = with_columns(side, new, f)
    side_ref[...] = side
    kt, ct = kt_ref[...], ct_ref[...]
    got = sums(1, t_row, t_lane, tk)
    third = iota((96, 256), 0) % 3
    columns = columns_in[...]
    for c in range(3):
        now = jnp.concatenate([str_ref[0, c, 0], str_ref[1, c, 0]], axis=1)
        own = kt * now
        pair = jnp.where(third == 0, pltpu.roll(own, 95, 0), jnp.where(third == 1, pltpu.roll(own, 1, 0), 0.0))
        new = pt_ref[c] + ct * got[c]
        load = got[3 + c] + got[6] * (own + pair) - kt * new
        for p in range(2):
            str1_ref[p, c] = new[:, p * 128 : p * 128 + 128]
            tload_ref[p, c] = load[:, p * 128 : p * 128 + 128]
            columns = with_columns(columns, new[:, p * 128 : p * 128 + 128], (p * 3 + c) * 6)
    last_ref[24:120, :] = columns
    first_ref[24:120, :] = columns


def bonds_body(
    stiff_ref, coef_ref, mat_ref, smat_ref, lefts_ref, rights_ref, before_ref, after_ref,
    sb_far, tb_far, sb_ref, tb_ref, sh_ref, th_ref, edge_ref, tedge_ref, sems,
):
    tabs = tables(stiff_ref, coef_ref)
    edge_ref[...] = joined(lefts_ref[...], rights_ref[...])
    tedge_ref[...] = joined(before_ref[24:120, :], after_ref[24:120, :])
    out = []

    def send(source, target):
        move = pltpu.make_async_copy(source, target, sems.at[len(out)])
        move.start()
        out.append(move)

    for l in range(6):
        for r0 in range(0, 128, CHUNK):
            sl = pl.ds(r0, CHUNK)
            half, coef = half_coef(mat_ref[l, sl, :], tabs)
            if l > 0:
                sb_ref[l - 1, 3, sl, :] = 1.0 / (half + sh_ref[l - 1, sl, :])
            sh_ref[l, sl, :] = half
            sb_ref[l, 4, sl, :] = coef
        layer_bonds(
            rows_of(sh_ref, l), 128, ends_of(before_ref, after_ref, 18 + l), edge_ref, 18 + l,
            sb_ref.at[l, 0], sb_ref.at[l, 1], sb_ref.at[l, 2],
        )
        if l > 0:
            send(sb_ref.at[l - 1], sb_far.at[l - 1])
    send(sb_ref.at[5], sb_far.at[5])
    for p in range(2):
        for t in range(6):
            for r0 in range(0, 96, CHUNK):
                sl = pl.ds(r0, CHUNK)
                half, coef = half_coef(smat_ref[p, t, sl, :], tabs)
                if t > 0:
                    tb_ref[p, t - 1, 3, sl, :] = 1.0 / (half + th_ref[t - 1, sl, :])
                th_ref[t, sl, :] = half
                tb_ref[p, t, 4, sl, :] = coef
            layer_bonds(
                rows_of(th_ref, t), 96, None, tedge_ref, 36 + p * 6 + t,
                tb_ref.at[p, t, 0], tb_ref.at[p, t, 1], tb_ref.at[p, t, 2],
            )
            if t > 0:
                send(tb_ref.at[p, t - 1], tb_far.at[p, t - 1])
        send(tb_ref.at[p, 5], tb_far.at[p, 5])
    finish(out)


def kinds(ref):
    return tuple((lambda l, k=k: ref.at[l, k]) for k in range(5))


def skin_layer(layer, now, prev, bonds, edge_ref, before_ref, after_ref, extra, put):
    for r0 in range(0, 128, CHUNK):
        chunk_step(
            now, prev, 128, r0, layer, 3, bonds, edge_ref, lambda c: c * 6 + layer,
            lambda c: ends_of(before_ref, after_ref, c * 6 + layer),
            None if extra is None else (lambda c: extra[c, pl.ds(r0, CHUNK), :]),
            lambda c, v: put(c, pl.ds(r0, CHUNK), v),
        )


def str_layer(p, layer, now, prev, bonds, edge_ref, extra, put):
    for r0 in range(0, 96, CHUNK):
        chunk_step(
            now, prev, 96, r0, layer, 3, bonds, edge_ref, lambda c: (p * 3 + c) * 6 + layer, None,
            None if extra is None else (lambda c: extra[p, c, pl.ds(r0, CHUNK), :]),
            lambda c, v: put(c, pl.ds(r0, CHUNK), v),
        )


def moving(pairs, sems):
    moves = {}
    for key, source, target in pairs:
        moves[key] = pltpu.make_async_copy(source, target, sems.at[len(moves)])
        moves[key].start()
    return moves


def first_skin_body(
    skin_far, prev_far, before_far, after_far, lefts_far, rights_far, sb_far, later_ref,
    skin1_far, last_ref, first_ref, side_ref,
    skin_ref, prev_ref, before_ref, after_ref, lefts_ref, rights_ref, sb_ref, skin1_ref, edge_ref, sems,
):
    pairs = [
        ("l", lefts_far, lefts_ref), ("r", rights_far, rights_ref), ("b", before_far, before_ref), ("a", after_far, after_ref),
    ]
    for l in range(6):
        pairs.append((("u", l), skin_far.at[:, l], skin_ref.at[:, l]))
        if l < 5:
            pairs += [(("k", l), sb_far.at[l], sb_ref.at[l]), (("v", l), prev_far.at[:, l], prev_ref.at[:, l])]
    moves = moving(pairs, sems)
    need = gate(moves)
    last_ref[...] = jnp.zeros((24, 128), F32)
    first_ref[...] = jnp.zeros((24, 128), F32)
    need("l", "r", "b", "a")
    edge_ref[...] = joined(lefts_ref[...], rights_ref[...])
    out = []
    for l in range(5):
        need(("u", l), ("u", l + 1), ("k", l), ("v", l))

        def put(c, sl, value):
            skin1_ref[c, l, sl, :] = value

        skin_layer(
            l, lambda c, m: rows_of(skin_ref, c, m), lambda c, m: rows_of(prev_ref, c, m), kinds(sb_ref), edge_ref,
            before_ref, after_ref, None, put,
        )
        out.append(pltpu.make_async_copy(skin1_ref.at[:, l], skin1_far.at[:, l], sems.at[len(pairs) + l]))
        out[l].start()
    for r0 in range(0, 128, CHUNK):
        side_ref[pl.ds(r0, CHUNK), :] = pack_skin(
            jnp.zeros((CHUNK, 128), F32), lambda c, l: skin1_ref[c, l, pl.ds(r0, CHUNK), :], range(5), r0, first_ref, last_ref
        )
    finish(out)


def first_str_body(
    str_far, prev_far, before_far, after_far, tb_far, later_ref,
    str1_far, columns_ref,
    str_ref, prev_ref, before_ref, after_ref, tb_ref, str1_ref, tedge_ref, sems,
):
    pairs = [("b", before_far, before_ref), ("a", after_far, after_ref)]
    for p in range(2):
        for t in range(6):
            pairs += [
                (("u", p, t), str_far.at[p, :, t], str_ref.at[p, :, t]), (("k", p, t), tb_far.at[p, t], tb_ref.at[p, t]),
            ]
            if t > 0:
                pairs.append((("v", p, t), prev_far.at[p, :, t], prev_ref.at[p, :, t]))
    moves = moving(pairs, sems)
    need = gate(moves)
    need("b", "a")
    tedge_ref[...] = joined(before_ref[24:120, :], after_ref[24:120, :])
    out = []
    for p in range(2):
        for t in range(1, 6):
            need(("u", p, t - 1), ("k", p, t - 1), ("u", p, t), ("u", p, t + 1), ("k", p, t), ("v", p, t))

            def put(c, sl, value):
                str1_ref[p, c, t - 1, sl, :] = value

            str_layer(
                p, t, lambda c, m: rows_of(str_ref, p, c, m), lambda c, m: rows_of(prev_ref, p, c, m),
                kinds(tb_ref.at[p]), tedge_ref, None, put,
            )
            move = pltpu.make_async_copy(
                str1_ref.at[p, :, t - 1], str1_far.at[p, :, t - 1], sems.at[len(pairs) + len(out)]
            )
            move.start()
            out.append(move)
    for r0 in range(0, 96, CHUNK):
        columns_ref[pl.ds(r0, CHUNK), :] = pack_str(
            jnp.zeros((CHUNK, 128), F32), lambda p, c, t: str1_ref[p, c, t - 1, pl.ds(r0, CHUNK), :], range(1, 6)
        )
    finish(out)


def second_body(
    skin_far, prev_far, str_far, str_prev_far, lefts_far, rights_far, before_far, after_far, sb_far, tb_far,
    skin_face_far, str_face_far, sload_far, tload_far,
    skin2_far, str2_far,
    skin_ref, prev_ref, str_ref, str_prev_ref, lefts_ref, rights_ref, before_ref, after_ref, sb_ref, tb_ref,
    skin_face_ref, str_face_ref, sload_ref, tload_ref,
    skin2_ref, str2_ref, edge_ref, tedge_ref, sems,
):
    pairs = [
        ("l", lefts_far, lefts_ref), ("r", rights_far, rights_ref), ("b", before_far, before_ref), ("a", after_far, after_ref),
    ]
    for l in range(6):
        if l < 5:
            pairs.append((("u", l), skin_far.at[:, l], skin_ref.at[:, l]))
        else:
            pairs += [(("u", l), skin_face_far, skin_face_ref), ("s", sload_far, sload_ref)]
        pairs += [(("k", l), sb_far.at[l], sb_ref.at[l]), (("v", l), prev_far.at[:, l], prev_ref.at[:, l])]
    pairs += [("f", str_face_far, str_face_ref), ("t", tload_far, tload_ref)]
    for p in range(2):
        for t in range(6):
            if t > 0:
                pairs.append((("u", p, t), str_far.at[p, :, t - 1], str_ref.at[p, :, t - 1]))
            pairs += [
                (("k", p, t), tb_far.at[p, t], tb_ref.at[p, t]),
                (("v", p, t), str_prev_far.at[p, :, t], str_prev_ref.at[p, :, t]),
            ]
    moves = moving(pairs, sems)
    need = gate(moves)
    need("l", "r", "b", "a")
    edge_ref[...] = joined(lefts_ref[...], rights_ref[...])
    tedge_ref[...] = joined(before_ref[24:120, :], after_ref[24:120, :])
    out = []

    def send(source, target):
        move = pltpu.make_async_copy(source, target, sems.at[len(pairs) + len(out)])
        move.start()
        out.append(move)

    for l in range(6):
        need(("u", l), ("u", l + 1), ("k", l), ("v", l))
        if l == 5:
            need("s")

        def put(c, sl, value):
            skin2_ref[c, l, sl, :] = value

        skin_layer(
            l, lambda c, m: rows_of(skin_face_ref, c) if m == 5 else rows_of(skin_ref, c, m),
            lambda c, m: rows_of(prev_ref, c, m), kinds(sb_ref), edge_ref, before_ref, after_ref,
            sload_ref if l == 5 else None, put,
        )
        send(skin2_ref.at[:, l], skin2_far.at[:, l])
    need("f", "t")
    for p in range(2):
        for t in range(6):
            need(("u", p, t), ("u", p, t + 1), ("k", p, t), ("v", p, t))

            def put(c, sl, value):
                str2_ref[p, c, t, sl, :] = value

            str_layer(
                p, t, lambda c, m: rows_of(str_face_ref, p, c) if m == 0 else rows_of(str_ref, p, c, m - 1),
                lambda c, m: rows_of(str_prev_ref, p, c, m), kinds(tb_ref.at[p]), tedge_ref,
                tload_ref if t == 0 else None, put,
            )
            send(str2_ref.at[p, :, t], str2_far.at[p, :, t])
    finish(out)


def swap(values):
    peers = lax.axis_size("chord")
    moved = lax.all_to_all(values.reshape(peers, -1, 128), "chord", split_axis=0, concat_axis=0, tiled=True)
    return moved.reshape(values.shape)


def shards(
    skin_now, skin_prev, skin_mat, stringer_now, stringer_prev, stringer_mat, owner_slot,
    rivet_span, rivet_chord, rivet_stringer, rivet_cell, rivet_stiff, mat_stiff, mat_coef,
):
    mats = [mat_stiff, mat_coef]
    own = [skin_now, skin_mat, stringer_now, stringer_mat]
    column = [(120, 128), (120, 128), (128, 128)]
    sent, match, *packs = call(
        opening_body, [(32, 128), (128, 128), *column],
        [*mats, rivet_span, rivet_chord, rivet_stringer, rivet_cell, rivet_stiff, owner_slot.reshape(1, -1), *own],
        "opening", smem=(0, 1), far=range(8, 12), flops=4000000, nbytes=4000000, scratch=near(own), sems=4,
    )
    rows = swap(sent)
    halos = exchange(*packs)
    edges = [(128, 128), (96, 128)]
    bonds = [(6, 5, 136, 128), (2, 6, 5, 104, 128)]
    bonds = call(
        bonds_body, bonds, [*mats, skin_mat, stringer_mat, *halos[2:], *halos[:2]], "bonds", smem=(0, 1), far_outs=(0, 1),
        flops=10000000, nbytes=8000000, scratch=floats(*bonds, (6, 128, 128), (6, 96, 128), *edges), sems=18,
    )
    found, *kept = call(
        gather_body, [(128, 128), (128, 128), (3, 128, 128), (128, 128), (96, 256), (3, 96, 256), (96, 256)],
        [*mats, rows, skin_now, skin_prev, skin_mat, stringer_now, stringer_prev, stringer_mat, *halos, bonds[0]], "gather",
        smem=(0, 1), far=(13,), flops=1000000000, nbytes=2000000,
        views={
            3: ((3, 2, 128, 128), (0, 2, 0, 0)),
            4: ((3, 1, 128, 128), (0, 5, 0, 0)),
            5: ((2, 128, 128), (2, 0, 0)),
            6: ((2, 3, 2, 96, 128), (0, 0, 0, 0, 0)),
            7: ((2, 3, 1, 96, 128), (0, 0, 0, 0, 0)),
            8: ((2, 2, 96, 128), (0, 0, 0, 0)),
        },
        scratch=floats((128, 128), (136, 128), (128, 128), (128, 128), (128, 128), *edges, (128, 128)),
    )
    given = swap(found)
    parts = [skin_now, skin_prev, *halos, bonds[0]]
    skin1, last, first, side = call(
        first_skin_body, [(3, 5, 128, 128), (24, 128), (24, 128), (128, 128)], [*parts, found], "first_skin",
        far=range(8), far_outs=(0,), flops=10000000, nbytes=5000000,
        scratch=near(parts) + floats((3, 5, 128, 128), (128, 128)), sems=25,
    )
    given, last, side = lax.optimization_barrier((given, last, side))
    (turned,) = call(bounce_body, [(128, 128)], [match, given], "bounce", fast=(1,), limit=8)
    posted = swap(turned)
    parts = [stringer_now, stringer_prev, *halos[:2], bonds[1]]
    str1, columns = call(
        first_str_body, [(2, 3, 5, 96, 128), (96, 128)], [*parts, turned], "first_str",
        far=range(6), far_outs=(0,), flops=10000000, nbytes=5000000,
        scratch=near(parts) + floats((2, 3, 5, 96, 128), (96, 128)), sems=46,
    )
    skin_face, sload, str_face, tload, *packs2 = call(
        load_body, [(3, 128, 128), (3, 128, 128), (2, 3, 96, 128), (2, 3, 96, 128), *column],
        [rows, posted, *kept, skin_now, stringer_now, last, first, side, columns], "load", flops=1000000000, nbytes=2000000,
        views={8: ((3, 1, 128, 128), (0, 5, 0, 0)), 9: ((2, 3, 1, 96, 128), (0, 0, 0, 0, 0))},
    )
    halos1 = exchange(*packs2)
    parts = [skin1, skin_now, str1, stringer_now, *halos1[2:], *halos1[:2], *bonds, skin_face, str_face, sload, tload]
    results = [(3, 6, 128, 128), (2, 3, 6, 96, 128)]
    return call(
        second_body, results, parts, "second", far=range(14), far_outs=(0, 1), flops=20000000, nbytes=10000000,
        scratch=near(parts) + floats(*results, *edges), sems=80, limit=56,
    )


def solution(mesh):
    placed = (
        P(None, None, "span", "chord"),
        P(None, None, "span", "chord"),
        P(None, "span", "chord"),
        P("chord", None, None, None, "span"),
        P("chord", None, None, None, "span"),
        P("chord", None, None, "span"),
        P(),
        P(("span", "chord")),
        P(("span", "chord")),
        P(("span", "chord")),
        P(("span", "chord")),
        P(("span", "chord")),
        P(),
        P(),
    )
    body = jax.shard_map(
        shards,
        mesh=mesh,
        in_specs=placed,
        out_specs=(P(None, None, "span", "chord"), P("chord", None, None, None, "span")),
        check_vma=False,
    )
    return lambda *args: tuple(body(*args))
```
